512 devices in a mesh: dp: 64 (over z_hi, y, core), seq: 8 (over z_lo, x).
Axes of the slice: x: 4, y: 8, z: 8 (z_hi: 4, z_lo: 2; z = z_hi * 2 + z_lo), core: 2. Of those that a mesh axis runs over, the one named last changes fastest.
Arguments:
- query_rows: bfloat16 [64, 1536, 2048], P('dp', 'seq'), may hold values from -6 to 6
- key_rows: bfloat16 [64, 1536, 2048], P('dp', 'seq'), may hold values from -6 to 6
- value_rows: bfloat16 [64, 1536, 2048], P('dp', 'seq'), may hold values from -6 to 6
- key_tiles: int32 [16, 4, 4], replicated, may hold values from 0 to 3, as said below
- tile_counts: int32 [16, 4], replicated, may hold values from 1 to 4
- out_weight: bfloat16 [2048, 3072], P('dp'), may hold values from -1.25 to 1.25
- gate_scale: bfloat16 [64, 3072], P('dp'), may hold values from 0.5 to 1.5
- residual: bfloat16 [64, 1536, 3072], P('dp', 'seq'), may hold values from -6 to 6
Outputs:
- block_out: bfloat16 [64, 1536, 3072], P('dp', 'seq')
The draws below stay inside these ranges and needn't reach their ends.
Inputs may be any that keep to these rules, and one draw needn't show every extreme that they name: Tiles form a grid of 2 frame positions by 2 height positions by 1 width positions; the tile at frame index a, height index b and width index c has the number a * 2 + b + c. The first tile_counts[h, s] entries of key_tiles[h, s, :] are, in increasing order, the distinct tiles of a box of this grid that contains tile s; the remaining entries equal s.
All inputs are finite; a program needn't handle non-finite values.
Results may differ from the reference program's by a relative error of at most 0.012.
Values may be sent and summed in bfloat16 or wider, within the bound.
A program may use at most 64 MiB of HBM per device.

```python
import math
import jax
import jax.numpy as jnp
from jax import lax

D = 3072
HD = 128
HEADS = 16
TILE = 384
GT = 2
GH = 2
GW = 1
NTILES = 4
SEQLEN = 1536
CLIPS = 64


def draw_query_rows(key, part):
    key = jax.random.fold_in(key, 11)
    drawn = jnp.clip(jax.random.normal(key, (CLIPS, SEQLEN, HEADS, HD)), -4.0, 4.0)
    return drawn.reshape(CLIPS, SEQLEN, HEADS * HD).astype(jnp.bfloat16)


def draw_key_rows(key, part):
    key = jax.random.fold_in(key, 12)
    drawn = jnp.clip(jax.random.normal(key, (CLIPS, SEQLEN, HEADS, HD)), -4.0, 4.0)
    return drawn.reshape(CLIPS, SEQLEN, HEADS * HD).astype(jnp.bfloat16)


def window_pattern(key):
    key = jax.random.fold_in(key, 707)
    lottery = jax.random.randint(jax.random.fold_in(key, 1), (HEADS, 3), 0, 10)
    grid_dims = jnp.array([GT, GH, GW], jnp.int32)
    radius = jnp.where(lottery < 6, 0, jnp.where(lottery < 8, 1, grid_dims[None, :] - 1))
    ranking = jax.random.permutation(jax.random.fold_in(key, 2), HEADS)
    radius = jnp.where((ranking == 0)[:, None], grid_dims[None, :] - 1, radius)
    radius = jnp.where((ranking == 1)[:, None], 0, radius)
    radius = jnp.minimum(radius, grid_dims[None, :] - 1)
    tile_ids = jnp.arange(NTILES, dtype=jnp.int32)
    coords = jnp.stack([tile_ids // (GH * GW), tile_ids // GW % GH, tile_ids % GW], axis=1)
    low_end = jnp.maximum(coords[None, :, :] - radius[:, None, :], 0)
    high_end = jnp.minimum(coords[None, :, :] + radius[:, None, :], grid_dims[None, None, :] - 1)
    extent = high_end - low_end + 1
    counted = extent[:, :, 0] * extent[:, :, 1] * extent[:, :, 2]
    slot_ids = jnp.arange(NTILES, dtype=jnp.int32)[None, None, :]
    step_frames = slot_ids // (extent[:, :, 1:2] * extent[:, :, 2:3])
    step_height = slot_ids // extent[:, :, 2:3] % extent[:, :, 1:2]
    step_width = slot_ids % extent[:, :, 2:3]
    listed = ((low_end[:, :, 0:1] + step_frames) * GH + low_end[:, :, 1:2] + step_height) * GW + low_end[:, :, 2:3] + step_width
    listed = jnp.where(slot_ids < counted[:, :, None], listed, tile_ids[None, :, None])
    return (listed.astype(jnp.int32), counted.astype(jnp.int32))


def draw_key_tiles(key, part):
    return window_pattern(key)[0]


def draw_tile_counts(key, part):
    return window_pattern(key)[1]


def steps_of(rng, shape, cuts, smallest, high):
    def one(axis_at, parts):
        heights = jax.random.uniform(jax.random.fold_in(jax.random.fold_in(rng, 6), axis_at), (parts,), jnp.float32, smallest / len(cuts), high / len(cuts))
        return jnp.repeat(jnp.exp(heights), shape[axis_at] // parts).reshape((-1,) + (1,) * (len(shape) - axis_at - 1))

    factor_of = one(*cuts[0])
    for cut in cuts[1:]:
        factor_of = factor_of * one(*cut)
    return factor_of


def gaussian(stream_key, shape, spread, bound, shards=(), held_as=jnp.bfloat16):
    result = spread * jax.random.normal(stream_key, shape, jnp.float32)
    if shards:
        result = result * steps_of(stream_key, shape, shards, -0.22, 0.18)
    return jnp.clip(result, -bound, bound).astype(held_as)


def setup_inputs(seed: int = 0) -> dict:
    arg_keys = jax.random.split(jax.random.key(seed), 9)
    query_rows = draw_query_rows(jax.random.fold_in(arg_keys[8], 71), 0)
    key_rows = draw_key_rows(jax.random.fold_in(arg_keys[8], 71), 0)
    value_rows = gaussian(arg_keys[2], (CLIPS, SEQLEN, HEADS * HD), 1.0, 6.0, ((0, 64), (1, 8)))
    key_tiles = draw_key_tiles(jax.random.fold_in(arg_keys[8], 71), 0)
    tile_counts = draw_tile_counts(jax.random.fold_in(arg_keys[8], 71), 0)
    out_weight = gaussian(arg_keys[5], (HEADS * HD, D), (HEADS * HD * 4 // TILE) ** -0.5, 1.25, ((0, 64),))
    gate_scale = jnp.clip(0.5 + 1.0 * jax.random.uniform(arg_keys[6], (CLIPS, D), jnp.float32) ** steps_of(arg_keys[6], (CLIPS, D), ((0, 64),), -0.2, 0.2), 0.5, 1.5).astype(jnp.bfloat16)
    residual = gaussian(arg_keys[7], (CLIPS, SEQLEN, D), 1.0, 6.0, ((0, 64), (1, 8)))
    return dict(query_rows=query_rows, key_rows=key_rows, value_rows=value_rows, key_tiles=key_tiles, tile_counts=tile_counts, out_weight=out_weight, gate_scale=gate_scale, residual=residual)


def head_attention(query_head, key_head, value_head, visible):
    allowed = jnp.repeat(jnp.repeat(visible, TILE, axis=0), TILE, axis=1)
    scores = jnp.dot(query_head, key_head.T, preferred_element_type=jnp.float32) * (1.0 / math.sqrt(HD))
    row_peak = lax.optimization_barrier(jnp.max(jnp.where(allowed, scores, -jnp.inf), axis=1, keepdims=True))
    shifted = jnp.where(allowed, jnp.exp(scores - row_peak), 0.0)
    row_total = lax.optimization_barrier(jnp.sum(shifted, axis=1, keepdims=True))
    mixed = jnp.dot(shifted.astype(jnp.bfloat16), value_head, preferred_element_type=jnp.float32) / row_total
    return mixed.astype(jnp.bfloat16)

def reference(query_rows, key_rows, value_rows, key_tiles, tile_counts, out_weight, gate_scale, residual):
    slot_ids = jnp.arange(NTILES, dtype=jnp.int32)
    listed = (key_tiles[:, :, :, None] == slot_ids[None, None, None, :]) & (slot_ids[None, None, :, None] < tile_counts[:, :, None, None])
    visible = jnp.any(listed, axis=2)

    def one_clip(inputs):
        query_clip, key_clip, value_clip, gate_clip, residual_clip = inputs

        def one_head(head_index):
            first_col = (head_index * HD).astype(jnp.int32)
            query_head = lax.dynamic_slice_in_dim(query_clip, first_col, HD, 1)
            key_head = lax.dynamic_slice_in_dim(key_clip, first_col, HD, 1)
            value_head = lax.dynamic_slice_in_dim(value_clip, first_col, HD, 1)
            head_mask = lax.dynamic_index_in_dim(visible, head_index, 0, keepdims=False)
            return head_attention(query_head, key_head, value_head, head_mask)
        per_head = lax.map(one_head, jnp.arange(HEADS, dtype=jnp.int32))
        attended = jnp.transpose(per_head, (1, 0, 2)).reshape(SEQLEN, HEADS * HD)
        projected = jnp.dot(attended, out_weight, preferred_element_type=jnp.float32)
        mixed_out = residual_clip.astype(jnp.float32) + gate_clip.astype(jnp.float32)[None, :] * projected
        return mixed_out.astype(jnp.bfloat16)
    return lax.map(one_clip, (query_rows, key_rows, value_rows, gate_scale, residual))
```

```python
import functools
import math

import jax
import jax.numpy as jnp
from jax import lax
from jax.experimental import pallas as pl
from jax.experimental.pallas import tpu as pltpu
from jax.sharding import PartitionSpec as P

MESH = pl.DeviceIdType.MESH

HEAD_DIM = 128
NX, NZ_LO = 4, 2
NY, NZ_HI, NCORE = 8, 4, 2
GROUP = NX * NZ_LO
SLOTS = 2
NTILES = 4
SHARED = 384
STEPS = ((4, 3, 4, 3), (3, 4, 3, 4))
ARRIVALS = tuple(
    tuple(
        (j, t) for pair in ((0, 1), (2, 3)) for t in range(4) for j in pair if t < STEPS[way][j]
    )
    for way in range(2)
)


def kernel(
    q_in, k_in, v_in, tiles, counts, w_in, gate_in, res_in, out,
    qb, kb, vb, stage, ob, wb, rb, gs, gb, outv,
    a_send, a_recv, a_loc, o_send, o_recv, o_loc, f_send, f_recv,
    y_send, y_recv, b_send, b_recv, z_send, z_recv, s_send, s_recv, s_loc, p_send, p_recv, p_loc,
):
    dp, me = lax.axis_index("dp"), lax.axis_index("seq")
    z_hi, y, core = dp // (NY * NCORE), (dp // NCORE) % NY, dp % NCORE
    z_lo, x = me // NX, me % NX
    way_z = 2 * z_lo - 1
    tok = q_in.shape[1]
    half = w_in.shape[1] // 2
    w_rows = w_in.shape[0]
    other = 1 - core

    sib = (dp + 1 - 2 * core, me)
    ring = tuple(
        (z_hi * NY * NCORE + ((y + d) % NY) * NCORE + core, me) for d in (1, NY - 1)
    )
    near = (((z_hi + way_z + NZ_HI) % NZ_HI) * NY * NCORE + y * NCORE + core, (1 - z_lo) * NX + x)
    twin = (dp, (1 - z_lo) * NX + x)

    def peer(i):
        return ((z_lo + i // NX) % NZ_LO) * NX + (x + i) % NX

    def block_at(zh, yy):
        return ((yy // 2) % 2) * 16 + (zh * 2 + yy // 4) * 2 + yy % 2

    def remote(src, dst, send, recv, to):
        return pltpu.make_async_remote_copy(
            src_ref=src, dst_ref=dst, send_sem=send, recv_sem=recv, device_id=to, device_id_type=MESH
        )

    def head_cols(p, slot):
        return pl.ds(pl.multiple_of((p * SLOTS + slot) * HEAD_DIM, HEAD_DIM), HEAD_DIM)

    mine = pl.ds(pl.multiple_of(core * half, 128), half)
    theirs = pl.ds(pl.multiple_of(other * half, 128), half)
    orders = tuple(
        (z_hi + NZ_HI + off) % NZ_HI for off in (0, way_z, -way_z, 2)
    )
    y_cols = pl.ds(pl.multiple_of(z_lo * SHARED, 128), half - SHARED)
    b_cols = pl.ds(pl.multiple_of(z_lo * (half - SHARED), 128), SHARED)
    b_cols_in = pl.ds(pl.multiple_of((1 - z_lo) * (half - SHARED), 128), SHARED)
    own_block = block_at(z_hi, y)

    w_local = pltpu.make_async_copy(
        w_in.at[:, mine], wb.at[own_block, pl.ds(core * w_rows, w_rows)], s_loc.at[0]
    )
    w_local.start()
    tensors = ((k_in, kb), (q_in, qb), (v_in, vb))

    def own_copy(n, slot):
        src, dst = tensors[n]
        return pltpu.make_async_copy(src.at[0, :, head_cols(me, slot)], dst.at[slot, me], a_loc.at[n, slot])

    for slot in range(SLOTS):
        for n in range(3):
            own_copy(n, slot).start()
    r_local = pltpu.make_async_copy(res_in.at[0, :, mine], rb.at[core], s_loc.at[1])
    r_local.start()
    gs[...] = jnp.broadcast_to(gate_in[...].astype(jnp.float32), gs.shape)
    g_local = pltpu.make_async_copy(gs.at[:, mine], gb.at[core], s_loc.at[2])
    g_local.start()

    barrier = pltpu.get_barrier_semaphore()
    for to in (sib, *ring, near):
        pl.semaphore_signal(barrier, inc=1, device_id=to, device_id_type=MESH)

    def greet(i, _):
        pl.semaphore_signal(barrier, inc=1, device_id=(dp, peer(i)), device_id_type=MESH)
        return 0

    lax.fori_loop(1, GROUP, greet, 0)
    pl.semaphore_wait(barrier, GROUP + 3)

    w_sib = remote(
        w_in.at[:, theirs],
        wb.at[own_block, pl.ds(core * w_rows, w_rows)],
        s_send.at[0], s_recv.at[0], sib,
    )
    w_sib.start()

    def send_copy(n, slot, p):
        src, dst = tensors[n]
        return remote(
            src.at[0, :, head_cols(p, slot)], dst.at[slot, me],
            a_send.at[n, slot, p], a_recv.at[n, slot, me], (dp, p),
        )

    def arrival(n, slot, p):
        src, dst = tensors[n]
        return remote(
            src.at[0, :, head_cols(p, slot)], dst.at[slot, p],
            a_send.at[n, slot, p], a_recv.at[n, slot, p], (dp, p),
        )

    def send_all(n, slot):
        def one(i, _):
            send_copy(n, slot, peer(i)).start()
            return 0

        lax.fori_loop(1, GROUP, one, 0)

    for n in range(3):
        send_all(n, 0)

    def z_copy(n):
        at = block_at(orders[(0, 1, 2)[n]], y)
        return remote(wb.at[at], wb.at[at], z_send.at[n], z_recv.at[n], (near, twin, near)[n])

    def z_arrival(n):
        at = block_at(orders[n + 1], y)
        return remote(wb.at[at], wb.at[at], z_send.at[n], z_recv.at[n], (near, twin, near)[n])

    def y_copy(way, at):
        view = wb.at[at, :, y_cols]
        return remote(view, view, y_send.at[way, at], y_recv.at[at], ring[way])

    def b_copy(at):
        view = wb.at[at, :, b_cols]
        return remote(view, view, b_send.at[at], b_recv.at[at], near)

    def b_arrival(at):
        view = wb.at[at, :, b_cols_in]
        return remote(view, view, b_send.at[at], b_recv.at[at], near)

    def y_first(j):
        at = block_at(orders[j], y)
        for way in range(2):
            y_copy(way, at).start()

    def y_round(e):
        for way in range(2):
            j, t = ARRIVALS[way][e]
            step = (NY - 1 - t) if way == 0 else t + 1
            at = block_at(orders[j], (y + step) % NY)
            y_copy(way, at).wait_recv()
            if t + 1 < STEPS[way][j]:
                y_copy(way, at).start()
            b_copy(at).start()

    w_local.wait()
    w_sib.wait_recv()
    z_copy(0).start()
    y_first(0)
    for n in range(3):
        send_all(n, 1)
    r_sib = remote(res_in.at[0, :, theirs], rb.at[core], s_send.at[1], s_recv.at[1], sib)
    r_sib.start()
    g_local.wait()
    g_sib = remote(gs.at[:, theirs], gb.at[core], s_send.at[2], s_recv.at[2], sib)
    g_sib.start()

    def z_done(n):
        z_arrival(n).wait_recv()
        if n < 2:
            z_copy(n + 1).start()
        y_first(n + 1)

    def o_copy(slot, p):
        return remote(
            stage.at[slot, p], ob.at[slot, core, :, pl.ds(pl.multiple_of(me * HEAD_DIM, HEAD_DIM), HEAD_DIM)],
            o_send.at[slot, p], o_recv.at[slot, me], (dp, p),
        )

    def o_arrival(slot, p):
        return remote(
            stage.at[slot, p], ob.at[slot, core, :, pl.ds(pl.multiple_of(p * HEAD_DIM, HEAD_DIM), HEAD_DIM)],
            o_send.at[slot, p], o_recv.at[slot, p], (dp, p),
        )

    def o_own(slot):
        return pltpu.make_async_copy(
            stage.at[slot, me],
            ob.at[slot, core, :, pl.ds(pl.multiple_of(me * HEAD_DIM, HEAD_DIM), HEAD_DIM)],
            o_loc.at[slot],
        )

    factor = math.log2(math.e) / math.sqrt(HEAD_DIM)
    per_tile = GROUP // NTILES
    tile = per_tile * tok

    def attend(slot, p):
        head = me * SLOTS + slot
        q_tile = p // per_tile
        count = counts[head, q_tile]
        listed = [tiles[head, q_tile, n] for n in range(NTILES)]
        queries = qb[slot, p]
        scores, peaks, seen = [], [], []
        for t in range(NTILES):
            keys = kb[slot, t * per_tile : (t + 1) * per_tile].reshape(tile, HEAD_DIM)
            s = lax.dot_general(
                queries, keys, (((1,), (1,)), ((), ())), preferred_element_type=jnp.float32
            )
            scores.append(s)
            peaks.append(jnp.max(s, axis=1, keepdims=True))
            hits = jnp.int32(0)
            for n in range(NTILES):
                hits = hits + jnp.where((listed[n] == t) & (n < count), 1, 0)
            seen.append(hits > 0)
        peak = None
        for t in range(NTILES):
            here = jnp.where(seen[t], peaks[t], -jnp.inf)
            peak = here if peak is None else jnp.maximum(peak, here)
        total, mixed = None, None
        for t in range(NTILES):
            shift = jnp.where(seen[t], peak * factor, jnp.inf)
            weights = jnp.exp2(scores[t] * factor - shift)
            values = vb[slot, t * per_tile : (t + 1) * per_tile].reshape(tile, HEAD_DIM)
            part = jnp.dot(weights.astype(jnp.bfloat16), values, preferred_element_type=jnp.float32)
            row = jnp.sum(weights, axis=1, keepdims=True)
            total = row if total is None else total + row
            mixed = part if mixed is None else mixed + part
        stage[slot, p] = (mixed / total).astype(jnp.bfloat16)

    def head_pass(slot, between):
        own_copy(0, slot).wait()
        own_copy(2, slot).wait()
        own_copy(1, slot).wait()

        def landed(i, _):
            arrival(0, slot, peer(i)).wait_recv()
            arrival(2, slot, peer(i)).wait_recv()
            return 0

        lax.fori_loop(1, GROUP, landed, 0)

        def one(i, _):
            p = peer(i)

            @pl.when(i > 0)
            def _():
                arrival(1, slot, p).wait_recv()

            attend(slot, p)

            @pl.when(i > 0)
            def _():
                o_copy(slot, p).start()

            for at, work in between.items():

                @pl.when(i == at)
                def _(work=work):
                    work()

            return 0

        lax.fori_loop(0, GROUP, one, 0)
        o_own(slot).start()

    def o_landed(slot):
        def one(i, _):
            o_arrival(slot, peer(i)).wait_recv()
            return 0

        lax.fori_loop(1, GROUP, one, 0)
        o_own(slot).wait()

    def forward(slot):
        view = ob.at[slot, core]
        return remote(view, view, f_send.at[slot], f_recv.at[slot], sib)

    def forwarded(slot):
        view = ob.at[slot, other]
        return remote(view, view, f_send.at[slot], f_recv.at[slot], sib)

    z_done(0)
    y_round(0)
    y_round(1)
    y_round(2)
    z_done(1)
    y_round(3)
    y_round(4)
    head_pass(0, {2: lambda: y_round(5), 5: lambda: (z_done(2), y_round(6))})
    y_round(7)
    y_round(8)
    head_pass(1, {2: lambda: y_round(9), 5: lambda: y_round(10)})
    o_landed(0)
    forward(0).start()
    y_round(11)
    o_landed(1)
    forward(1).start()
    y_round(12)
    y_round(13)
    r_local.wait()
    r_sib.wait_recv()
    g_sib.wait_recv()

    def blocks_done(u, _):
        at = block_at(u // (NY - 1), (y + 1 + u % (NY - 1)) % NY)
        b_arrival(at).wait_recv()
        return 0

    lax.fori_loop(0, NZ_HI * (NY - 1), blocks_done, 0)
    forwarded(0).wait_recv()
    forwarded(1).wait_recv()

    wide = outv.shape[3]
    parts = outv.shape[0]

    def out_cols(n):
        return pl.ds(pl.multiple_of(core * half + n * wide, 128), wide)

    def out_own(n):
        return pltpu.make_async_copy(outv.at[n, core], out.at[0, :, out_cols(n)], p_loc.at[n])

    def out_sib(n):
        return remote(outv.at[n, other], out.at[0, :, out_cols(n)], p_send.at[n], p_recv.at[n], sib)

    def out_sib_in(n):
        cols = pl.ds(pl.multiple_of(other * half + n * wide, 128), wide)
        return remote(outv.at[n, other], out.at[0, :, cols], p_send.at[n], p_recv.at[n], sib)

    per_slot = wb.shape[0] // SLOTS
    depth = per_slot * wb.shape[1]

    def project(n, _):
        cols = pl.ds(pl.multiple_of(n * wide, 128), wide)
        acc = None
        for slot in range(SLOTS):
            part = jnp.dot(
                ob[slot].reshape(NCORE * tok, depth),
                wb[slot * per_slot : (slot + 1) * per_slot, :, cols].reshape(depth, wide),
                preferred_element_type=jnp.float32,
            )
            acc = part if acc is None else acc + part
        for clip in range(NCORE):
            rows = acc[clip * tok : (clip + 1) * tok]
            mixed = rb[clip, :, cols].astype(jnp.float32) + gb[clip, 0:1, cols] * rows
            outv[n, clip] = mixed.astype(jnp.bfloat16)
        out_own(n).start()
        out_sib(n).start()
        return 0

    lax.fori_loop(0, parts, project, 0)

    for slot in range(SLOTS):
        for n in range(3):

            def sent(i, _, n=n, slot=slot):
                send_copy(n, slot, peer(i)).wait_send()
                return 0

            lax.fori_loop(1, GROUP, sent, 0)

        def o_sent(i, _, slot=slot):
            o_copy(slot, peer(i)).wait_send()
            return 0

        lax.fori_loop(1, GROUP, o_sent, 0)
        forward(slot).wait_send()
    for n in range(3):
        z_copy(n).wait_send()
    for way in range(2):
        for j in range(NZ_HI):
            for t in range(STEPS[way][j]):
                step = (NY - t) if way == 0 else t
                y_copy(way, block_at(orders[j], (y + step) % NY)).wait_send()

    def b_sent(u, _):
        at = block_at(u // (NY - 1), (y + 1 + u % (NY - 1)) % NY)
        b_copy(at).wait_send()
        return 0

    lax.fori_loop(0, NZ_HI * (NY - 1), b_sent, 0)
    w_sib.wait_send()
    r_sib.wait_send()
    g_sib.wait_send()

    def out_done(n, _):
        out_own(n).wait()
        out_sib(n).wait_send()
        out_sib_in(n).wait_recv()
        return 0

    lax.fori_loop(0, parts, out_done, 0)


def on_device(
    query_rows, key_rows, value_rows, key_tiles, tile_counts, out_weight, gate_scale, residual
):
    tok, feats = query_rows.shape[1:]
    w_rows, width = out_weight.shape
    half = width // NCORE
    parts = 6
    bf16, f32 = jnp.bfloat16, jnp.float32
    dma = pltpu.SemaphoreType.DMA
    blocks = NZ_HI * NY
    hbm = pl.BlockSpec(memory_space=pl.ANY)
    smem = pl.BlockSpec(memory_space=pltpu.SMEM)
    vmem = pl.BlockSpec(memory_space=pltpu.VMEM)
    return pl.pallas_call(
        kernel,
        out_shape=jax.ShapeDtypeStruct(residual.shape, residual.dtype),
        in_specs=[hbm, hbm, hbm, smem, smem, hbm, vmem, hbm],
        out_specs=hbm,
        scratch_shapes=[
            pltpu.VMEM((SLOTS, GROUP, tok, HEAD_DIM), bf16),
            pltpu.VMEM((SLOTS, GROUP, tok, HEAD_DIM), bf16),
            pltpu.VMEM((SLOTS, GROUP, tok, HEAD_DIM), bf16),
            pltpu.VMEM((SLOTS, GROUP, tok, HEAD_DIM), bf16),
            pltpu.VMEM((SLOTS, NCORE, tok, feats // SLOTS), bf16),
            pltpu.VMEM((blocks, NCORE * w_rows, half), bf16),
            pltpu.VMEM((NCORE, tok, half), bf16),
            pltpu.VMEM((8, width), f32),
            pltpu.VMEM((NCORE, 8, half), f32),
            pltpu.VMEM((parts, NCORE, tok, half // parts), bf16),
            dma((3, SLOTS, GROUP)),
            dma((3, SLOTS, GROUP)),
            dma((3, SLOTS)),
            dma((SLOTS, GROUP)),
            dma((SLOTS, GROUP)),
            dma((SLOTS,)),
            dma((SLOTS,)),
            dma((SLOTS,)),
            dma((2, blocks)),
            dma((blocks,)),
            dma((blocks,)),
            dma((blocks,)),
            dma((3,)),
            dma((3,)),
            dma((3,)),
            dma((3,)),
            dma((3,)),
            dma((parts,)),
            dma((parts,)),
            dma((parts,)),
        ],
        compiler_params=pltpu.CompilerParams(
            collective_id=0, has_side_effects=True, vmem_limit_bytes=56 << 20
        ),
    )(query_rows, key_rows, value_rows, key_tiles, tile_counts, out_weight, gate_scale, residual)


def solution(mesh):
    in_specs = (
        P("dp", "seq", None),
        P("dp", "seq", None),
        P("dp", "seq", None),
        P(),
        P(),
        P("dp", None),
        P("dp", None),
        P("dp", "seq", None),
    )
    return jax.shard_map(
        on_device, mesh=mesh, in_specs=in_specs, out_specs=P("dp", "seq", None), check_vma=False
    )
```

```python
import functools
import math

import jax
import jax.numpy as jnp
from jax import lax
from jax.experimental import pallas as pl
from jax.experimental.pallas import tpu as pltpu
from jax.sharding import PartitionSpec as P

MESH = pl.DeviceIdType.MESH

HEAD_DIM = 128
NX, NZ_LO = 4, 2
NY, NZ_HI, NCORE = 8, 4, 2
GROUP = NX * NZ_LO
SLOTS = 2
NTILES = 4
SHARED = 384
STEPS = ((4, 3, 4, 3), (3, 4, 3, 4))
ARRIVALS = (
    ((0, 0), (1, 0), (0, 1), (2, 0), (1, 1), (0, 2), (3, 0), (2, 1), (1, 2), (3, 1), (0, 3), (2, 2), (3, 2), (2, 3)),
    ((0, 0), (1, 0), (0, 1), (2, 0), (1, 1), (0, 2), (3, 0), (1, 2), (3, 1), (2, 1), (3, 2), (1, 3), (2, 2), (3, 3)),
)


def kernel(
    q_in, k_in, v_in, tiles, counts, w_in, gate_in, res_in, out,
    qb, kb, vb, stage, ob, wb, rb, gs, gb, sums, outv,
    a_send, a_recv, a_loc, o_send, o_recv, o_loc, f_send, f_recv, y_send, y_recv, x_send, x_recv,
    b_send, b_recv, z_send, z_recv, s_send, s_recv, s_loc, p_send, p_recv, p_loc,
):
    dp, me = lax.axis_index("dp"), lax.axis_index("seq")
    z_hi, y, core = dp // (NY * NCORE), (dp // NCORE) % NY, dp % NCORE
    z_lo, x = me // NX, me % NX
    way_z = 2 * z_lo - 1
    tok = q_in.shape[1]
    half = w_in.shape[1] // 2
    other = 1 - core

    sib = (dp + 1 - 2 * core, me)
    ring = tuple(
        (z_hi * NY * NCORE + ((y + d) % NY) * NCORE + core, me) for d in (1, NY - 1)
    )
    near = (((z_hi + way_z + NZ_HI) % NZ_HI) * NY * NCORE + y * NCORE + core, (1 - z_lo) * NX + x)
    twin = (dp, (1 - z_lo) * NX + x)
    beside = tuple((dp, z_lo * NX + (x + d) % NX) for d in (1, NX - 1))
    kept, skipped = 1 - x % 2, x % 2

    def peer(i):
        return ((z_lo + i // NX) % NZ_LO) * NX + (x + i) % NX

    def block_at(zh, yy):
        return ((yy // 2) % 2) * 16 + (zh * 2 + yy // 4) * 2 + yy % 2

    def shard_at(zh, yy, part):
        return block_at(zh, yy) * NCORE + (core + part) % NCORE

    def remote(src, dst, send, recv, to):
        return pltpu.make_async_remote_copy(
            src_ref=src, dst_ref=dst, send_sem=send, recv_sem=recv, device_id=to, device_id_type=MESH
        )

    def all_sent(view, sem):
        remote(view, view, sem, sem, sib).wait_send()

    def all_landed(view, sem):
        remote(view, view, sem, sem, sib).wait_recv()

    def head_cols(p, slot):
        return pl.ds(pl.multiple_of((p * SLOTS + slot) * HEAD_DIM, HEAD_DIM), HEAD_DIM)

    mine = pl.ds(pl.multiple_of(core * half, 128), half)
    theirs = pl.ds(pl.multiple_of(other * half, 128), half)
    orders = tuple(
        (z_hi + NZ_HI + off) % NZ_HI for off in (0, way_z, -way_z, 2)
    )
    y_cols = pl.ds(pl.multiple_of(z_lo * SHARED, 128), half - SHARED)
    b_cols = pl.ds(pl.multiple_of(z_lo * (half - SHARED), 128), SHARED)
    b_cols_in = pl.ds(pl.multiple_of((1 - z_lo) * (half - SHARED), 128), SHARED)
    own_shard = shard_at(z_hi, y, 0)

    w_local = pltpu.make_async_copy(
        w_in.at[:, mine], wb.at[own_shard], s_loc.at[0]
    )
    w_local.start()
    tensors = ((k_in, kb), (q_in, qb), (v_in, vb))

    def own_copy(n, slot):
        src, dst = tensors[n]
        return pltpu.make_async_copy(src.at[0, :, head_cols(me, slot)], dst.at[slot, me], a_loc.at[slot])

    for slot in range(SLOTS):
        for n in range(3):
            own_copy(n, slot).start()
    r_local = pltpu.make_async_copy(res_in.at[0, :, mine], rb.at[core], s_loc.at[1])
    r_local.start()
    gs[...] = jnp.broadcast_to(gate_in[...].astype(jnp.float32), gs.shape)
    g_local = pltpu.make_async_copy(gs.at[:, mine], gb.at[core], s_loc.at[2])
    g_local.start()

    barrier = pltpu.get_barrier_semaphore()
    for to in (sib, *ring, near):
        pl.semaphore_signal(barrier, inc=1, device_id=to, device_id_type=MESH)

    def greet(i, _):
        pl.semaphore_signal(barrier, inc=1, device_id=(dp, peer(i)), device_id_type=MESH)
        return 0

    lax.fori_loop(1, GROUP, greet, 0)
    pl.semaphore_wait(barrier, GROUP + 3)

    w_sib = remote(
        w_in.at[:, theirs],
        wb.at[own_shard],
        s_send.at[0], s_recv.at[0], sib,
    )
    w_sib.start()

    def send_all(slot, lo, hi):
        for n in range(3):
            src, dst = tensors[n]

            def one(i, _, n=n, src=src, dst=dst):
                p = peer(i)
                if n == 1:
                    done = a_recv.at[slot, 1 + i // NX]
                else:
                    done = a_recv.at[slot, 0]
                remote(
                    src.at[0, :, head_cols(p, slot)], dst.at[slot, me], a_send.at[n], done, (dp, p)
                ).start()
                return 0

            lax.fori_loop(lo, hi, one, 0)

    def z_copy(n, part):
        view = wb.at[shard_at(orders[n], y, part)]
        return remote(view, view, z_send, z_recv.at[n, part], (near, twin, near)[n])

    def z_arrival(n, part):
        view = wb.at[shard_at(orders[n + 1], y, part)]
        return remote(view, view, z_send, z_recv.at[n, part], (near, twin, near)[n])

    def y_copy(way, at):
        view = wb.at[at, :, y_cols]
        return remote(view, view, y_send, y_recv.at[at], ring[way])

    def x_copy(way, t, at):
        view = wb.at[at, :, y_cols]
        return remote(view, view, x_send, x_recv.at[way, t], beside[way])

    def b_copy(j, at):
        view = wb.at[at, :, b_cols]
        return remote(view, view, b_send, b_recv.at[j // 2], near)

    def y_first(j, part):
        at = shard_at(orders[j], y, part)
        for way in range(2):
            y_copy(way, at).start()

    def row_of(way, t):
        return (y + ((NY - 1 - t) if way == 0 else t + 1)) % NY

    def y_round(e):
        for part in range(NCORE):
            for way in range(2):
                j, t = ARRIVALS[way][e]
                if j == 3 and part:
                    continue
                at = shard_at(orders[j], row_of(way, t), kept if j == 3 else part)
                y_copy(way, at).wait_recv()
                if t + 1 < STEPS[way][j]:
                    y_copy(way, at).start()
                if j == 3:
                    x_copy(way, t, at).start()
                b_copy(j, at).start()

    def x_done(way, t):
        at = shard_at(orders[3], row_of(way, t), skipped)
        x_copy(way, t, at).wait_recv()
        b_copy(3, at).start()

    def z_done(n):
        for part in range(NCORE):
            z_arrival(n, part).wait_recv()
            if n < 2:
                z_copy(n + 1, part).start()
                y_first(n + 1, part)
        if n == 2:
            y_first(3, kept)

    w_local.wait()
    z_copy(0, 0).start()
    y_first(0, 0)
    send_all(0, 1, NX)
    w_sib.wait_recv()
    z_copy(0, 1).start()
    y_first(0, 1)
    r_sib = remote(res_in.at[0, :, theirs], rb.at[core], s_send.at[1], s_recv.at[1], sib)
    r_sib.start()
    g_local.wait()
    g_sib = remote(gs.at[:, theirs], gb.at[core], s_send.at[2], s_recv.at[2], sib)
    g_sib.start()

    def o_copy(slot, p):
        return remote(
            stage.at[slot, p], ob.at[slot, core, :, pl.ds(pl.multiple_of(me * HEAD_DIM, HEAD_DIM), HEAD_DIM)],
            o_send, o_recv.at[slot], (dp, p),
        )

    def o_own(slot):
        return pltpu.make_async_copy(
            stage.at[slot, me],
            ob.at[slot, core, :, pl.ds(pl.multiple_of(me * HEAD_DIM, HEAD_DIM), HEAD_DIM)],
            o_loc.at[slot],
        )

    factor = math.log2(math.e) / math.sqrt(HEAD_DIM)
    per_tile = GROUP // NTILES
    tile = per_tile * tok

    def attend(slot, p):
        head = me * SLOTS + slot
        q_tile = p // per_tile
        count = counts[q_tile, head]
        listed = [tiles[q_tile, n, head] for n in range(NTILES)]
        queries = qb[slot, p]
        scores, peaks, seen = [], [], []
        for t in range(NTILES):
            keys = kb[slot, t * per_tile : (t + 1) * per_tile].reshape(tile, HEAD_DIM)
            s = lax.dot_general(
                queries, keys, (((1,), (1,)), ((), ())), preferred_element_type=jnp.float32
            )
            scores.append(s)
            peaks.append(jnp.max(s, axis=1, keepdims=True))
            hits = jnp.int32(0)
            for n in range(NTILES):
                hits = hits + jnp.where((listed[n] == t) & (n < count), 1, 0)
            seen.append(hits > 0)
        peak = None
        for t in range(NTILES):
            here = jnp.where(seen[t], peaks[t], -jnp.inf)
            peak = here if peak is None else jnp.maximum(peak, here)
        total, mixed = None, None
        for t in range(NTILES):
            shift = jnp.where(seen[t], peak * factor, jnp.inf)
            weights = jnp.exp2(scores[t] * factor - shift)
            values = vb[slot, t * per_tile : (t + 1) * per_tile].reshape(tile, HEAD_DIM)
            part = jnp.dot(weights.astype(jnp.bfloat16), values, preferred_element_type=jnp.float32)
            row = jnp.sum(weights, axis=1, keepdims=True)
            total = row if total is None else total + row
            mixed = part if mixed is None else mixed + part
        stage[slot, p] = (mixed / total).astype(jnp.bfloat16)

    def head_pass(slot, between):
        here = qb.at[0, 0:3]
        pltpu.make_async_copy(here, here, a_loc.at[slot]).wait()
        all_landed(kb.at[0:2, 0 : GROUP - 1], a_recv.at[slot, 0])

        def one(i, _):
            p = peer(i)

            @pl.when(i == 1)
            def _():
                all_landed(qb.at[slot, 0 : NX - 1], a_recv.at[slot, 1])

            @pl.when(i == NX)
            def _():
                all_landed(qb.at[slot, 0:NX], a_recv.at[slot, 2])

            attend(slot, p)

            @pl.when(i > 0)
            def _():
                o_copy(slot, p).start()

            for at, work in between.items():

                @pl.when(i == at)
                def _(work=work):
                    work()

            return 0

        lax.fori_loop(0, GROUP, one, 0)
        o_own(slot).start()

    def o_landed(slot):
        all_landed(stage.at[slot, 0 : GROUP - 1], o_recv.at[slot])
        o_own(slot).wait()

    def forward(slot):
        view = ob.at[slot, core]
        return remote(view, view, f_send, f_recv, sib)

    z_done(0)
    send_all(0, NX, GROUP)
    send_all(1, 1, GROUP)
    y_round(0)
    y_round(1)
    z_done(1)
    y_round(2)
    y_round(3)
    z_done(2)
    y_round(4)
    head_pass(0, {2: lambda: y_round(5), 5: lambda: y_round(6)})
    y_round(7)
    y_round(8)
    x_done(0, 0)
    x_done(1, 0)
    y_round(9)
    head_pass(1, {2: lambda: y_round(10), 5: lambda: y_round(11)})
    x_done(0, 1)
    x_done(1, 1)
    o_landed(0)
    forward(0).start()
    y_round(12)
    x_done(1, 2)
    o_landed(1)
    forward(1).start()
    y_round(13)
    x_done(0, 2)
    x_done(1, 3)
    r_local.wait()
    r_sib.wait_recv()
    g_sib.wait_recv()
    all_landed(ob.at[:, 0], f_recv)

    wide = outv.shape[3]
    parts = outv.shape[0]

    def out_cols(n):
        return pl.ds(pl.multiple_of(core * half + n * wide, 128), wide)

    def out_own(n):
        return pltpu.make_async_copy(outv.at[n, core], out.at[0, :, out_cols(n)], p_loc)

    def out_sib(n):
        return remote(outv.at[n, other], out.at[0, :, out_cols(n)], p_send, p_recv, sib)

    per_slot = wb.shape[0] // SLOTS
    per_zh = per_slot // NZ_HI
    depth = per_zh * wb.shape[1]

    def products(pair, cols):
        acc = None
        for j in pair:
            zh = orders[j]
            feats = pl.ds(pl.multiple_of(zh * depth, 128), depth)
            for slot in range(SLOTS):
                part = jnp.dot(
                    ob[slot, :, :, feats].reshape(NCORE * tok, depth),
                    wb[pl.ds(slot * per_slot + zh * per_zh, per_zh), :, cols].reshape(depth, wide),
                    preferred_element_type=jnp.float32,
                )
                acc = part if acc is None else acc + part
        return acc

    def early(n, _):
        sums[n] = products((0, 1), pl.ds(pl.multiple_of(n * wide, 128), wide))
        return 0

    def late(n, _):
        cols = pl.ds(pl.multiple_of(n * wide, 128), wide)
        acc = sums[n] + products((2, 3), cols)
        for clip in range(NCORE):
            rows = acc[clip * tok : (clip + 1) * tok]
            mixed = rb[clip, :, cols].astype(jnp.float32) + gb[clip, 0:1, cols] * rows
            outv[n, clip] = mixed.astype(jnp.bfloat16)
        out_own(n).start()
        out_sib(n).start()
        return 0

    half_far = NCORE * NZ_HI * (NY - 1) // 2
    all_landed(wb.at[0:half_far, :, 0:SHARED], b_recv.at[0])
    lax.fori_loop(0, parts, early, 0)
    all_landed(wb.at[0:half_far, :, 0:SHARED], b_recv.at[1])
    lax.fori_loop(0, parts, late, 0)

    for n in range(3):
        all_sent(kb.at[0:2, 0 : GROUP - 1], a_send.at[n])
    all_sent(stage.at[0:2, 0 : GROUP - 1], o_send)
    all_sent(ob.at[:, 0], f_send)
    all_sent(wb.at[0 : 3 * NCORE], z_send)
    all_sent(wb.at[0 : (NCORE * NZ_HI - 1) * (NY - 1), :, 0 : half - SHARED], y_send)
    all_sent(wb.at[0 : NY - 1, :, 0 : half - SHARED], x_send)
    all_sent(wb.at[0 : 2 * half_far, :, 0:SHARED], b_send)
    w_sib.wait_send()
    r_sib.wait_send()
    g_sib.wait_send()
    pltpu.make_async_copy(outv.at[:, 0], outv.at[:, 0], p_loc).wait()
    all_sent(outv.at[:, 0], p_send)
    all_landed(outv.at[:, 0], p_recv)


def on_device(
    query_rows, key_rows, value_rows, key_tiles, tile_counts, out_weight, gate_scale, residual
):
    tok, feats = query_rows.shape[1:]
    w_rows, width = out_weight.shape
    half = width // NCORE
    parts = 6
    bf16, f32 = jnp.bfloat16, jnp.float32
    dma = pltpu.SemaphoreType.DMA
    shards = NZ_HI * NY * NCORE
    hbm = pl.BlockSpec(memory_space=pltpu.HBM)
    smem = pl.BlockSpec(memory_space=pltpu.SMEM)
    vmem = pl.BlockSpec(memory_space=pltpu.VMEM)
    return pl.pallas_call(
        kernel,
        out_shape=jax.ShapeDtypeStruct(residual.shape, residual.dtype),
        in_specs=[hbm, hbm, hbm, smem, smem, hbm, vmem, hbm],
        out_specs=pl.BlockSpec(memory_space=pl.ANY),
        scratch_shapes=[
            pltpu.VMEM((SLOTS, GROUP, tok, HEAD_DIM), bf16),
            pltpu.VMEM((SLOTS, GROUP, tok, HEAD_DIM), bf16),
            pltpu.VMEM((SLOTS, GROUP, tok, HEAD_DIM), bf16),
            pltpu.VMEM((SLOTS, GROUP, tok, HEAD_DIM), bf16),
            pltpu.VMEM((SLOTS, NCORE, tok, feats // SLOTS), bf16),
            pltpu.VMEM((shards, w_rows, half), bf16),
            pltpu.VMEM((NCORE, tok, half), bf16),
            pltpu.VMEM((8, width), f32),
            pltpu.VMEM((NCORE, 8, half), f32),
            pltpu.VMEM((parts, NCORE * tok, half // parts), f32),
            pltpu.VMEM((parts, NCORE, tok, half // parts), bf16),
            dma((3,)),
            dma((SLOTS, 3)),
            dma((SLOTS,)),
            dma,
            dma((SLOTS,)),
            dma((SLOTS,)),
            dma,
            dma,
            dma,
            dma((shards,)),
            dma,
            dma((2, 4)),
            dma,
            dma((2,)),
            dma,
            dma((3, NCORE)),
            dma((3,)),
            dma((3,)),
            dma((3,)),
            dma,
            dma,
            dma,
        ],
        compiler_params=pltpu.CompilerParams(
            collective_id=0, has_side_effects=True, vmem_limit_bytes=56 << 20
        ),
    )(
        query_rows, key_rows, value_rows, jnp.transpose(key_tiles, (1, 2, 0)), tile_counts.T,
        out_weight, gate_scale, residual,
    )


def solution(mesh):
    in_specs = (
        P("dp", "seq", None),
        P("dp", "seq", None),
        P("dp", "seq", None),
        P(),
        P(),
        P("dp", None),
        P("dp", None),
        P("dp", "seq", None),
    )
    return jax.shard_map(
        on_device, mesh=mesh, in_specs=in_specs, out_specs=P("dp", "seq", None), check_vma=False
    )
```

```python
import functools
import math

import jax
import jax.numpy as jnp
from jax import lax
from jax.experimental import pallas as pl
from jax.experimental.pallas import tpu as pltpu
from jax.sharding import PartitionSpec as P

MESH = pl.DeviceIdType.MESH

HEAD_DIM = 128
NX, NZ_LO = 4, 2
NY, NZ_HI, NCORE = 8, 4, 2
GROUP = NX * NZ_LO
SLOTS = 2
NTILES = 4
SHARED = 384
STEPS = ((4, 3, 4, 3), (3, 4, 3, 4))
BESIDE = 1
ORDER = (
    (("y", 0, 0, 0, 0), ("y", 1, 0, 0, 0), ("z", 0, 0), ("y", 0, 0, 1, 0), ("y", 1, 0, 1, 0), ("z", 0, 1),
     ("y", 0, 0, 0, 1), ("y", 1, 0, 0, 1), ("z", 1, 0), ("y", 0, 1, 0, 0), ("y", 1, 1, 0, 0), ("z", 1, 1),
     ("y", 0, 0, 1, 1), ("y", 1, 0, 1, 1), ("y", 0, 0, 0, 2), ("y", 1, 0, 0, 2), ("z", 2, 0),
     ("y", 0, 2, 0, 0), ("y", 1, 2, 0, 0), ("y", 0, 1, 0, 1), ("y", 1, 1, 0, 1), ("z", 2, 1),
     ("y", 0, 2, 1, 0), ("y", 1, 2, 1, 0), ("y", 0, 0, 1, 2), ("y", 1, 0, 1, 2),),
    (("y", 0, 0, 0, 3), ("y", 1, 3, 0, 0),),
    (("y", 0, 3, 0, 0), ("y", 1, 2, 0, 1),),
    (("y", 0, 2, 0, 1), ("y", 1, 1, 0, 2), ("y", 0, 1, 0, 2), ("y", 1, 3, 1, 0),),
    (("y", 0, 3, 1, 0), ("y", 1, 2, 1, 1), ("y", 0, 2, 1, 1), ("y", 1, 3, 0, 1), ("y", 0, 0, 1, 3),
     ("y", 1, 2, 0, 2), ("x", 0, 0), ("x", 1, 0), ("y", 0, 3, 0, 1), ("y", 1, 1, 0, 3), ("x", 0, 1),
     ("x", 1, 1),),
    (("y", 0, 2, 0, 2), ("y", 1, 3, 1, 1),),
    (("y", 0, 3, 1, 1), ("y", 1, 2, 1, 2),),
    (("y", 0, 2, 1, 2), ("y", 1, 3, 0, 2), ("x", 1, 2), ("x", 0, 2), ("y", 0, 3, 0, 2), ("y", 1, 3, 1, 2),),
    (("x", 1, 3), ("y", 0, 2, 0, 3), ("y", 1, 3, 0, 3), ("y", 0, 3, 1, 2), ("y", 1, 3, 1, 3),
     ("y", 0, 2, 1, 3),),
)


def kernel(
    q_in, k_in, v_in, tiles, counts, w_in, gate_in, res_in, out,
    qb, kb, vb, stage, ob, wb, rb, gs, gb, sums, outv,
    a_send, a_recv, a_loc, o_send, o_recv, o_loc, f_send, f_recv, y_send, y_recv, x_send, x_recv,
    b_send, b_recv, z_send, z_recv, s_send, s_recv, s_loc, p_send, p_recv, p_loc,
):
    dp, me = lax.axis_index("dp"), lax.axis_index("seq")
    z_hi, y, core = dp // (NY * NCORE), (dp // NCORE) % NY, dp % NCORE
    z_lo, x = me // NX, me % NX
    way_z = 2 * z_lo - 1
    tok = q_in.shape[1]
    half = w_in.shape[1] // 2
    other = 1 - core

    sib = (dp + 1 - 2 * core, me)
    ring = tuple(
        (z_hi * NY * NCORE + ((y + d) % NY) * NCORE + core, me) for d in (1, NY - 1)
    )
    near = (((z_hi + way_z + NZ_HI) % NZ_HI) * NY * NCORE + y * NCORE + core, (1 - z_lo) * NX + x)
    twin = (dp, (1 - z_lo) * NX + x)
    beside = tuple((dp, z_lo * NX + (x + d) % NX) for d in (1, NX - 1))
    kept, skipped = 1 - x % 2, x % 2

    def peer(i):
        return ((z_lo + i // NX) % NZ_LO) * NX + (x + i) % NX

    def block_at(zh, yy):
        return ((yy // 2) % 2) * 16 + (zh * 2 + yy // 4) * 2 + yy % 2

    def shard_at(zh, yy, part):
        return block_at(zh, yy) * NCORE + (core + part) % NCORE

    def remote(src, dst, send, recv, to):
        return pltpu.make_async_remote_copy(
            src_ref=src, dst_ref=dst, send_sem=send, recv_sem=recv, device_id=to, device_id_type=MESH
        )

    def all_sent(view, sem):
        remote(view, view, sem, sem, sib).wait_send()

    def all_landed(view, sem):
        remote(view, view, sem, sem, sib).wait_recv()

    def head_cols(p, slot):
        return pl.ds(pl.multiple_of((p * SLOTS + slot) * HEAD_DIM, HEAD_DIM), HEAD_DIM)

    mine = pl.ds(pl.multiple_of(core * half, 128), half)
    theirs = pl.ds(pl.multiple_of(other * half, 128), half)
    orders = tuple(
        (z_hi + NZ_HI + off) % NZ_HI for off in (0, way_z, -way_z, 2)
    )
    y_cols = pl.ds(pl.multiple_of(z_lo * SHARED, 128), half - SHARED)
    b_cols = pl.ds(pl.multiple_of(z_lo * (half - SHARED), 128), SHARED)
    b_cols_in = pl.ds(pl.multiple_of((1 - z_lo) * (half - SHARED), 128), SHARED)
    own_shard = shard_at(z_hi, y, 0)

    w_local = pltpu.make_async_copy(
        w_in.at[:, mine], wb.at[own_shard], s_loc.at[0]
    )
    w_local.start()
    tensors = ((k_in, kb), (v_in, vb), (q_in, qb))

    def own_copy(n, slot):
        src, dst = tensors[n]
        return pltpu.make_async_copy(src.at[0, :, head_cols(me, slot)], dst.at[slot, me], a_loc.at[slot])

    for slot in range(SLOTS):
        for n in range(3):
            own_copy(n, slot).start()
    r_local = pltpu.make_async_copy(res_in.at[0, :, mine], rb.at[core], s_loc.at[1])
    r_local.start()
    gs[...] = jnp.broadcast_to(gate_in[...].astype(jnp.float32), gs.shape)
    g_local = pltpu.make_async_copy(gs.at[:, mine], gb.at[core], s_loc.at[2])
    g_local.start()

    barrier = pltpu.get_barrier_semaphore()
    for to in (sib, *ring, near):
        pl.semaphore_signal(barrier, inc=1, device_id=to, device_id_type=MESH)

    def greet(i, _):
        pl.semaphore_signal(barrier, inc=1, device_id=(dp, peer(i)), device_id_type=MESH)
        return 0

    lax.fori_loop(1, GROUP, greet, 0)
    pl.semaphore_wait(barrier, GROUP + 3)

    w_sib = remote(
        w_in.at[:, theirs],
        wb.at[own_shard],
        s_send.at[0], s_recv.at[0], sib,
    )
    w_sib.start()

    def send_all(slot, lo, hi):
        for n in range(3):
            src, dst = tensors[n]

            def one(i, _, n=n, src=src, dst=dst):
                p = peer(i)
                if n == 2:
                    done = a_recv.at[slot, 1 + i // NX]
                else:
                    done = a_recv.at[slot, 0]
                remote(
                    src.at[0, :, head_cols(p, slot)], dst.at[slot, me], a_send.at[n], done, (dp, p)
                ).start()
                return 0

            lax.fori_loop(lo, hi, one, 0)

    def z_copy(n, part):
        view = wb.at[shard_at(orders[n], y, part)]
        return remote(view, view, z_send, z_recv.at[n, part], (near, twin, near)[n])

    def z_arrival(n, part):
        view = wb.at[shard_at(orders[n + 1], y, part)]
        return remote(view, view, z_send, z_recv.at[n, part], (near, twin, near)[n])

    def y_copy(way, at):
        view = wb.at[at, :, y_cols]
        return remote(view, view, y_send, y_recv.at[at], ring[way])

    def x_copy(way, t, at):
        view = wb.at[at, :, y_cols]
        return remote(view, view, x_send, x_recv.at[way, t], beside[way])

    def b_copy(j, at):
        view = wb.at[at, :, b_cols]
        return remote(view, view, b_send, b_recv.at[j // 2], near)

    def shard_of(j, yy, part):
        return shard_at(orders[j], yy, kept if j == BESIDE else part)

    def y_first(j, part):
        if j == BESIDE and part:
            return
        at = shard_of(j, y, part)
        for way in range(2):
            y_copy(way, at).start()

    def row_of(way, t):
        return (y + ((NY - 1 - t) if way == 0 else t + 1)) % NY

    def y_done(way, j, part, t):
        at = shard_of(j, row_of(way, t), part)
        y_copy(way, at).wait_recv()
        if t + 1 < STEPS[way][j]:
            y_copy(way, at).start()
        if j == BESIDE:
            x_copy(way, t, at).start()
        b_copy(j, at).start()

    def x_done(way, t):
        at = shard_at(orders[BESIDE], row_of(way, t), skipped)
        x_copy(way, t, at).wait_recv()
        b_copy(BESIDE, at).start()

    def z_done(n, part):
        z_arrival(n, part).wait_recv()
        if n < 2:
            z_copy(n + 1, part).start()
        if n + 1 != BESIDE:
            y_first(n + 1, part)
        elif part:
            y_first(n + 1, 0)
        if n == 0 and part:
            send_all(0, NX, GROUP)
            send_all(1, 1, GROUP)

    steps = {"z": z_done, "y": y_done, "x": x_done}

    def take(group):
        for name, *where in ORDER[group]:
            steps[name](*where)

    w_local.wait()
    z_copy(0, 0).start()
    y_first(0, 0)
    send_all(0, 1, NX)
    w_sib.wait_recv()
    z_copy(0, 1).start()
    y_first(0, 1)
    r_sib = remote(res_in.at[0, :, theirs], rb.at[core], s_send.at[1], s_recv.at[1], sib)
    r_sib.start()
    g_local.wait()
    g_sib = remote(gs.at[:, theirs], gb.at[core], s_send.at[2], s_recv.at[2], sib)
    g_sib.start()

    def o_copy(slot, p):
        return remote(
            stage.at[slot, p], ob.at[slot, core, :, pl.ds(pl.multiple_of(me * HEAD_DIM, HEAD_DIM), HEAD_DIM)],
            o_send, o_recv.at[slot], (dp, p),
        )

    def o_own(slot):
        return pltpu.make_async_copy(
            stage.at[slot, me],
            ob.at[slot, core, :, pl.ds(pl.multiple_of(me * HEAD_DIM, HEAD_DIM), HEAD_DIM)],
            o_loc.at[slot],
        )

    factor = math.log2(math.e) / math.sqrt(HEAD_DIM)
    per_tile = GROUP // NTILES
    tile = per_tile * tok

    def attend(slot, q_tile):
        head = me * SLOTS + slot
        count = counts[q_tile, head]
        listed = [tiles[q_tile, n, head] for n in range(NTILES)]
        first = q_tile * per_tile
        queries = qb[slot, pl.ds(first, per_tile)].reshape(tile, HEAD_DIM)
        scores, peaks, seen = [], [], []
        for t in range(NTILES):
            keys = kb[slot, t * per_tile : (t + 1) * per_tile].reshape(tile, HEAD_DIM)
            s = lax.dot_general(
                queries, keys, (((1,), (1,)), ((), ())), preferred_element_type=jnp.float32
            )
            scores.append(s)
            peaks.append(jnp.max(s, axis=1, keepdims=True))
            hits = jnp.int32(0)
            for n in range(NTILES):
                hits = hits + jnp.where((listed[n] == t) & (n < count), 1, 0)
            seen.append(hits > 0)
        peak = None
        for t in range(NTILES):
            here = jnp.where(seen[t], peaks[t], -jnp.inf)
            peak = here if peak is None else jnp.maximum(peak, here)
        total, mixed = None, None
        for t in range(NTILES):
            shift = jnp.where(seen[t], peak * factor, jnp.inf)
            weights = jnp.exp2(scores[t] * factor - shift)
            values = vb[slot, t * per_tile : (t + 1) * per_tile].reshape(tile, HEAD_DIM)
            part = jnp.dot(weights.astype(jnp.bfloat16), values, preferred_element_type=jnp.float32)
            row = jnp.sum(weights, axis=1, keepdims=True)
            total = row if total is None else total + row
            mixed = part if mixed is None else mixed + part
        done = (mixed / total).astype(jnp.bfloat16)
        stage[slot, pl.ds(first, per_tile)] = done.reshape(per_tile, tok, HEAD_DIM)

    def part_of_heads(g, _):
        slot, c = g // NTILES, g % NTILES

        @pl.when(c == 0)
        def _():
            here = qb.at[0, 0:3]
            pltpu.make_async_copy(here, here, a_loc.at[slot]).wait()
            all_landed(kb.at[0:2, 0 : GROUP - 1], a_recv.at[slot, 0])
            all_landed(qb.at[0, 0 : NX - 1], a_recv.at[slot, 1])

        @pl.when(c == NTILES // 2)
        def _():
            all_landed(qb.at[0, 0:NX], a_recv.at[slot, 2])

        q_tile = ((z_lo + c // 2) % NZ_LO) * (NTILES // NZ_LO) + (x // per_tile + c) % (NTILES // NZ_LO)
        attend(slot, q_tile)
        for n in range(per_tile):
            p = q_tile * per_tile + n

            @pl.when(p != me)
            def _(p=p):
                o_copy(slot, p).start()

        for group in range(SLOTS * NTILES):

            @pl.when(g == group)
            def _(group=group):
                if group % NTILES == 0:
                    o_own(group // NTILES).start()
                if group == SLOTS * NTILES - 1:
                    o_landed(0)
                    forward(0).start()
                take(group + 1)

        return 0

    def o_landed(slot):
        all_landed(stage.at[slot, 0 : GROUP - 1], o_recv.at[slot])
        o_own(slot).wait()

    def forward(slot):
        view = ob.at[slot, core]
        return remote(view, view, f_send, f_recv.at[slot], sib)

    take(0)
    lax.fori_loop(0, SLOTS * NTILES, part_of_heads, 0)
    r_local.wait()
    r_sib.wait_recv()
    g_sib.wait_recv()

    wide = outv.shape[3]
    parts = outv.shape[0]

    def out_cols(n):
        return pl.ds(pl.multiple_of(core * half + n * wide, 128), wide)

    def out_own(n):
        return pltpu.make_async_copy(outv.at[n, core], out.at[0, :, out_cols(n)], p_loc)

    def out_sib(n):
        return remote(outv.at[n, other], out.at[0, :, out_cols(n)], p_send, p_recv, sib)

    per_slot = wb.shape[0] // SLOTS
    per_zh = per_slot // NZ_HI
    depth = per_zh * wb.shape[1]

    def products(slots, places, cols):
        acc = None
        for j in places:
            zh = orders[j]
            feats = pl.ds(pl.multiple_of(zh * depth, 128), depth)
            for slot in slots:
                part = jnp.dot(
                    ob[slot, :, :, feats].reshape(NCORE * tok, depth),
                    wb[pl.ds(slot * per_slot + zh * per_zh, per_zh), :, cols].reshape(depth, wide),
                    preferred_element_type=jnp.float32,
                )
                acc = part if acc is None else acc + part
        return acc

    def early(n, _):
        sums[n] = products((0,), (0, 1), pl.ds(pl.multiple_of(n * wide, 128), wide))
        return 0

    def middle(n, _):
        sums[n] += products((1,), (0, 1), pl.ds(pl.multiple_of(n * wide, 128), wide))
        return 0

    def late(n, _):
        cols = pl.ds(pl.multiple_of(n * wide, 128), wide)
        acc = sums[n] + products((0, 1), (2, 3), cols)
        for clip in range(NCORE):
            rows = acc[clip * tok : (clip + 1) * tok]
            mixed = rb[clip, :, cols].astype(jnp.float32) + gb[clip, 0:1, cols] * rows
            outv[n, clip] = mixed.astype(jnp.bfloat16)
        out_own(n).start()
        out_sib(n).start()
        return 0

    half_far = NCORE * NZ_HI * (NY - 1) // 2
    all_landed(wb.at[0:half_far, :, 0:SHARED], b_recv.at[0])
    all_landed(ob.at[0, 0], f_recv.at[0])
    lax.fori_loop(0, parts, early, 0)
    o_landed(1)
    forward(1).start()
    all_landed(ob.at[0, 0], f_recv.at[1])
    lax.fori_loop(0, parts, middle, 0)
    all_landed(wb.at[0:half_far, :, 0:SHARED], b_recv.at[1])
    lax.fori_loop(0, parts, late, 0)

    for n in range(3):
        all_sent(kb.at[0:2, 0 : GROUP - 1], a_send.at[n])
    all_sent(stage.at[0:2, 0 : GROUP - 1], o_send)
    all_sent(ob.at[:, 0], f_send)
    all_sent(wb.at[0 : 3 * NCORE], z_send)
    all_sent(wb.at[0 : (NCORE * NZ_HI - 1) * (NY - 1), :, 0 : half - SHARED], y_send)
    all_sent(wb.at[0 : NY - 1, :, 0 : half - SHARED], x_send)
    all_sent(wb.at[0 : 2 * half_far, :, 0:SHARED], b_send)
    w_sib.wait_send()
    r_sib.wait_send()
    g_sib.wait_send()
    pltpu.make_async_copy(outv.at[:, 0], outv.at[:, 0], p_loc).wait()
    all_sent(outv.at[:, 0], p_send)
    all_landed(outv.at[:, 0], p_recv)


def on_device(
    query_rows, key_rows, value_rows, key_tiles, tile_counts, out_weight, gate_scale, residual
):
    tok, feats = query_rows.shape[1:]
    w_rows, width = out_weight.shape
    half = width // NCORE
    parts = 6
    bf16, f32 = jnp.bfloat16, jnp.float32
    dma = pltpu.SemaphoreType.DMA
    shards = NZ_HI * NY * NCORE
    hbm = pl.BlockSpec(memory_space=pltpu.HBM)
    smem = pl.BlockSpec(memory_space=pltpu.SMEM)
    vmem = pl.BlockSpec(memory_space=pltpu.VMEM)
    return pl.pallas_call(
        kernel,
        out_shape=jax.ShapeDtypeStruct(residual.shape, residual.dtype),
        in_specs=[hbm, hbm, hbm, smem, smem, hbm, vmem, hbm],
        out_specs=pl.BlockSpec(memory_space=pl.ANY),
        scratch_shapes=[
            pltpu.VMEM((SLOTS, GROUP, tok, HEAD_DIM), bf16),
            pltpu.VMEM((SLOTS, GROUP, tok, HEAD_DIM), bf16),
            pltpu.VMEM((SLOTS, GROUP, tok, HEAD_DIM), bf16),
            pltpu.VMEM((SLOTS, GROUP, tok, HEAD_DIM), bf16),
            pltpu.VMEM((SLOTS, NCORE, tok, feats // SLOTS), bf16),
            pltpu.VMEM((shards, w_rows, half), bf16),
            pltpu.VMEM((NCORE, tok, half), bf16),
            pltpu.VMEM((8, width), f32),
            pltpu.VMEM((NCORE, 8, half), f32),
            pltpu.VMEM((parts, NCORE * tok, half // parts), f32),
            pltpu.VMEM((parts, NCORE, tok, half // parts), bf16),
            dma((3,)),
            dma((SLOTS, 3)),
            dma((SLOTS,)),
            dma,
            dma((SLOTS,)),
            dma((SLOTS,)),
            dma,
            dma((SLOTS,)),
            dma,
            dma((shards,)),
            dma,
            dma((2, 4)),
            dma,
            dma((2,)),
            dma,
            dma((3, NCORE)),
            dma((3,)),
            dma((3,)),
            dma((3,)),
            dma,
            dma,
            dma,
        ],
        compiler_params=pltpu.CompilerParams(
            collective_id=0, has_side_effects=True, vmem_limit_bytes=56 << 20
        ),
    )(
        query_rows, key_rows, value_rows, jnp.transpose(key_tiles, (1, 2, 0)), tile_counts.T,
        out_weight, gate_scale, residual,
    )


def solution(mesh):
    in_specs = (
        P("dp", "seq", None),
        P("dp", "seq", None),
        P("dp", "seq", None),
        P(),
        P(),
        P("dp", None),
        P("dp", None),
        P("dp", "seq", None),
    )
    return jax.shard_map(
        on_device, mesh=mesh, in_specs=in_specs, out_specs=P("dp", "seq", None), check_vma=False
    )
```

```python
import functools
import math

import jax
import jax.numpy as jnp
from jax import lax
from jax.experimental import pallas as pl
from jax.experimental.pallas import tpu as pltpu
from jax.sharding import PartitionSpec as P

MESH = pl.DeviceIdType.MESH

HEAD_DIM = 128
NX, NZ_LO = 4, 2
NY, NZ_HI, NCORE = 8, 4, 2
GROUP = NX * NZ_LO
SLOTS = 2
NTILES = 4
SHARED = 384
STEPS = ((4, 3, 4, 3), (3, 4, 3, 4))
LAST = 0
BESIDE = 1
ORDER = (
    (("y", 0, 0, 0, 0), ("y", 1, 0, 0, 0), ("z", 0, 0), ("y", 0, 0, 1, 0), ("y", 1, 0, 1, 0), ("z", 0, 1), ("f", 1, 0),
     ("y", 0, 0, 0, 1), ("y", 1, 0, 0, 1), ("z", 1, 0), ("f", 2, 0), ("y", 0, 1, 0, 0), ("y", 1, 1, 0, 0), ("z", 1, 1), ("f", 2, 1),
     ("y", 0, 0, 1, 1), ("y", 1, 0, 1, 1), ("y", 0, 0, 0, 2), ("y", 1, 0, 0, 2), ("z", 2, 0), ("f", 3, 0),
     ("y", 0, 2, 0, 0), ("y", 1, 2, 0, 0), ("y", 0, 1, 0, 1), ("y", 1, 1, 0, 1), ("z", 2, 1), ("f", 3, 1),
     ("y", 0, 2, 1, 0), ("y", 1, 2, 1, 0), ("y", 0, 0, 1, 2), ("y", 1, 0, 1, 2),),
    (("y", 0, 0, 0, 3), ("y", 1, 3, 0, 0),),
    (("y", 0, 3, 0, 0), ("y", 1, 2, 0, 1),),
    (("y", 0, 2, 0, 1), ("y", 1, 1, 0, 2), ("y", 0, 1, 0, 2), ("y", 1, 3, 1, 0),),
    (("y", 0, 3, 1, 0), ("y", 1, 2, 1, 1), ("y", 0, 2, 1, 1), ("y", 1, 3, 0, 1), ("y", 0, 0, 1, 3),
     ("y", 1, 2, 0, 2), ("x", 0, 0), ("x", 1, 0), ("y", 0, 3, 0, 1), ("y", 1, 1, 0, 3), ("x", 0, 1),
     ("x", 1, 1),),
    (("y", 0, 2, 0, 2), ("y", 1, 3, 1, 1),),
    (("y", 0, 3, 1, 1), ("y", 1, 2, 1, 2),),
    (("y", 0, 2, 1, 2), ("y", 1, 3, 0, 2), ("x", 1, 2), ("x", 0, 2), ("y", 0, 3, 0, 2), ("y", 1, 3, 1, 2),),
    (("x", 1, 3), ("y", 0, 2, 0, 3), ("y", 1, 3, 0, 3), ("y", 0, 3, 1, 2), ("y", 1, 3, 1, 3),
     ("y", 0, 2, 1, 3),),
)


def kernel(
    q_in, k_in, v_in, tiles_in, counts_in, w_in, gate_in, res_in, out,
    tiles, counts, qb, kb, vb, stage, ob, wb, rb, gs, gb, outv,
    a_send, a_recv, a_loc, o_send, o_recv, o_loc, f_send, f_recv, y_send, y_recv, x_send, x_recv,
    b_send, b_recv, z_send, z_recv, s_send, s_recv, s_loc, t_loc, p_send, p_recv, p_loc,
):
    dp, me = lax.axis_index("dp"), lax.axis_index("seq")
    z_hi, y, core = dp // (NY * NCORE), (dp // NCORE) % NY, dp % NCORE
    z_lo, x = me // NX, me % NX
    way_z = 2 * z_lo - 1
    tok = q_in.shape[1]
    half = w_in.shape[1] // 2
    other = 1 - core

    sib = (dp + 1 - 2 * core, me)
    ring = tuple(
        (z_hi * NY * NCORE + ((y + d) % NY) * NCORE + core, me) for d in (1, NY - 1)
    )
    near = (((z_hi + way_z + NZ_HI) % NZ_HI) * NY * NCORE + y * NCORE + core, (1 - z_lo) * NX + x)
    twin = (dp, (1 - z_lo) * NX + x)
    beside = tuple((dp, z_lo * NX + (x + d) % NX) for d in (1, NX - 1))
    kept, skipped = 1 - x % 2, x % 2

    def peer(i):
        return ((z_lo + i // NX) % NZ_LO) * NX + (x + i) % NX

    def block_at(zh, yy):
        return ((yy // 2) % 2) * 16 + (zh * 2 + yy // 4) * 2 + yy % 2

    def shard_at(zh, yy, part):
        return block_at(zh, yy) * NCORE + (core + part) % NCORE

    def remote(src, dst, send, recv, to):
        return pltpu.make_async_remote_copy(
            src_ref=src, dst_ref=dst, send_sem=send, recv_sem=recv, device_id=to, device_id_type=MESH
        )

    def all_sent(view, sem):
        remote(view, view, sem, sem, sib).wait_send()

    def all_landed(view, sem):
        remote(view, view, sem, sem, sib).wait_recv()

    def head_cols(p, slot):
        return pl.ds(pl.multiple_of((p * SLOTS + slot) * HEAD_DIM, HEAD_DIM), HEAD_DIM)

    mine = pl.ds(pl.multiple_of(core * half, 128), half)
    theirs = pl.ds(pl.multiple_of(other * half, 128), half)
    orders = tuple(
        (z_hi + NZ_HI + off) % NZ_HI for off in (0, way_z, -way_z, 2)
    )
    y_cols = pl.ds(pl.multiple_of(z_lo * SHARED, 128), half - SHARED)
    b_cols = pl.ds(pl.multiple_of(z_lo * (half - SHARED), 128), SHARED)
    b_cols_in = pl.ds(pl.multiple_of((1 - z_lo) * (half - SHARED), 128), SHARED)
    own_shard = shard_at(z_hi, y, 0)

    barrier = pltpu.get_barrier_semaphore()
    for to in (sib, *ring, near):
        pl.semaphore_signal(barrier, inc=1, device_id=to, device_id_type=MESH)

    def greet(i, _):
        pl.semaphore_signal(barrier, inc=1, device_id=(dp, peer(i)), device_id_type=MESH)
        return 0

    lax.fori_loop(1, GROUP, greet, 0)
    w_local = pltpu.make_async_copy(
        w_in.at[:, mine], wb.at[own_shard], s_loc.at[0]
    )
    w_local.start()
    tensors = ((k_in, kb), (v_in, vb), (q_in, qb))

    def own_copy(n, slot):
        src, dst = tensors[n]
        return pltpu.make_async_copy(src.at[0, :, head_cols(me, slot)], dst.at[slot, me], a_loc.at[slot])

    for slot in range(SLOTS):
        for n in range(3):
            own_copy(n, slot).start()
    t_local = pltpu.make_async_copy(tiles_in, tiles, t_loc.at[0])
    c_local = pltpu.make_async_copy(counts_in, counts, t_loc.at[1])
    t_local.start()
    c_local.start()
    r_local = pltpu.make_async_copy(res_in.at[0, :, mine], rb.at[core], s_loc.at[1])
    r_local.start()
    gs[...] = jnp.broadcast_to(gate_in[...].astype(jnp.float32), gs.shape)
    g_local = pltpu.make_async_copy(gs.at[:, mine], gb.at[core], s_loc.at[2])
    g_local.start()

    pl.semaphore_wait(barrier, GROUP + 3)

    w_sib = remote(
        w_in.at[:, theirs],
        wb.at[own_shard],
        s_send.at[0], s_recv.at[0], sib,
    )
    w_sib.start()

    def send_all(slot, lo, hi):
        for n in range(3):
            src, dst = tensors[n]

            def one(i, _, n=n, src=src, dst=dst):
                p = peer(i)
                if n == 2:
                    done = a_recv.at[slot, 1 + i // NX]
                else:
                    done = a_recv.at[slot, 0]
                remote(
                    src.at[0, :, head_cols(p, slot)], dst.at[slot, me], a_send.at[n], done, (dp, p)
                ).start()
                return 0

            lax.fori_loop(lo, hi, one, 0)

    def z_copy(n, part):
        view = wb.at[shard_at(orders[n], y, part)]
        return remote(view, view, z_send, z_recv.at[n, part], (near, twin, near)[n])

    def z_arrival(n, part):
        view = wb.at[shard_at(orders[n + 1], y, part)]
        return remote(view, view, z_send, z_recv.at[n, part], (near, twin, near)[n])

    def y_copy(way, at):
        view = wb.at[at, :, y_cols]
        return remote(view, view, y_send, y_recv.at[at], ring[way])

    def x_copy(way, t, at):
        view = wb.at[at, :, y_cols]
        return remote(view, view, x_send, x_recv.at[way, t], beside[way])

    def b_copy(at):
        view = wb.at[at, :, b_cols]
        return remote(view, view, b_send, b_recv, near)

    def shard_of(j, yy, part):
        return shard_at(orders[j], yy, kept if j == BESIDE else part)

    def y_first(j, part):
        at = shard_of(j, y, part)
        for way in range(2):
            y_copy(way, at).start()

    def row_of(way, t):
        return (y + ((NY - 1 - t) if way == 0 else t + 1)) % NY

    def y_done(way, j, part, t):
        at = shard_of(j, row_of(way, t), part)
        y_copy(way, at).wait_recv()
        if t + 1 < STEPS[way][j]:
            y_copy(way, at).start()
        if j == BESIDE:
            x_copy(way, t, at).start()
        b_copy(at).start()

    def x_done(way, t):
        at = shard_at(orders[BESIDE], row_of(way, t), skipped)
        x_copy(way, t, at).wait_recv()
        b_copy(at).start()

    def z_done(n, part):
        z_arrival(n, part).wait_recv()
        if n < 2:
            z_copy(n + 1, part).start()
        if n == 0 and part:
            send_all(0, NX, GROUP)
            send_all(1, 1, GROUP)

    steps = {"f": y_first, "z": z_done, "y": y_done, "x": x_done}

    def take(group):
        for name, *where in group:
            steps[name](*where)

    w_local.wait()
    z_copy(0, 0).start()
    y_first(0, 0)
    send_all(0, 1, NX)
    w_sib.wait_recv()
    z_copy(0, 1).start()
    y_first(0, 1)
    r_sib = remote(res_in.at[0, :, theirs], rb.at[core], s_send.at[1], s_recv.at[1], sib)
    r_sib.start()
    g_local.wait()
    g_sib = remote(gs.at[:, theirs], gb.at[core], s_send.at[2], s_recv.at[2], sib)
    g_sib.start()

    def o_copy(slot, p):
        return remote(
            stage.at[slot, p], ob.at[slot, core, :, pl.ds(pl.multiple_of(me * HEAD_DIM, HEAD_DIM), HEAD_DIM)],
            o_send, o_recv.at[slot], (dp, p),
        )

    def o_own(slot):
        return pltpu.make_async_copy(
            stage.at[slot, me],
            ob.at[slot, core, :, pl.ds(pl.multiple_of(me * HEAD_DIM, HEAD_DIM), HEAD_DIM)],
            o_loc.at[slot],
        )

    factor = math.log2(math.e) / math.sqrt(HEAD_DIM)
    per_tile = GROUP // NTILES
    tile = per_tile * tok

    def attend(slot, q_tile):
        head = me * SLOTS + slot
        count = counts[q_tile, head]
        listed = [tiles[q_tile, n, head] for n in range(NTILES)]
        first = q_tile * per_tile
        queries = qb[slot, pl.ds(first, per_tile)].reshape(tile, HEAD_DIM)
        scores, peaks, seen = [], [], []
        for t in range(NTILES):
            keys = kb[slot, t * per_tile : (t + 1) * per_tile].reshape(tile, HEAD_DIM)
            s = lax.dot_general(
                queries, keys, (((1,), (1,)), ((), ())), preferred_element_type=jnp.float32
            )
            scores.append(s)
            peaks.append(jnp.max(s, axis=1, keepdims=True))
            hits = jnp.int32(0)
            for n in range(NTILES):
                hits = hits + jnp.where((listed[n] == t) & (n < count), 1, 0)
            seen.append(hits > 0)
        peak = None
        for t in range(NTILES):
            here = jnp.where(seen[t], peaks[t], -jnp.inf)
            peak = here if peak is None else jnp.maximum(peak, here)
        total, mixed = None, None
        for t in range(NTILES):
            shift = jnp.where(seen[t], peak * factor, jnp.inf)
            weights = jnp.exp2(scores[t] * factor - shift)
            values = vb[slot, t * per_tile : (t + 1) * per_tile].reshape(tile, HEAD_DIM)
            part = jnp.dot(weights.astype(jnp.bfloat16), values, preferred_element_type=jnp.float32)
            row = jnp.sum(weights, axis=1, keepdims=True)
            total = row if total is None else total + row
            mixed = part if mixed is None else mixed + part
        done = (mixed / total).astype(jnp.bfloat16)
        stage[slot, pl.ds(first, per_tile)] = done.reshape(per_tile, tok, HEAD_DIM)

    def part_of_heads(g, _):
        slot, c = g // NTILES, g % NTILES

        @pl.when(c == 0)
        def _():
            here = qb.at[0, 0:3]
            pltpu.make_async_copy(here, here, a_loc.at[slot]).wait()
            all_landed(kb.at[0:2, 0 : GROUP - 1], a_recv.at[slot, 0])
            all_landed(qb.at[0, 0 : NX - 1], a_recv.at[slot, 1])

        @pl.when(c == NTILES // 2)
        def _():
            all_landed(qb.at[0, 0:NX], a_recv.at[slot, 2])

        q_tile = ((z_lo + c // 2) % NZ_LO) * (NTILES // NZ_LO) + (x // per_tile + c) % (NTILES // NZ_LO)
        attend(slot, q_tile)
        for n in range(per_tile):
            p = q_tile * per_tile + n

            @pl.when(p != me)
            def _(p=p):
                o_copy(slot, p).start()

        for group in range(SLOTS * NTILES):

            @pl.when(g == group)
            def _(group=group):
                if group % NTILES == 0:
                    o_own(group // NTILES).start()
                if group < SLOTS * NTILES - 1:
                    take(ORDER[group + 1])

        return 0

    def o_landed(slot):
        all_landed(stage.at[slot, 0 : GROUP - 1], o_recv.at[slot])
        o_own(slot).wait()

    def forward(slot):
        view = ob.at[slot, core]
        return remote(view, view, f_send, f_recv, sib)

    take(ORDER[0])
    t_local.wait()
    c_local.wait()
    lax.fori_loop(0, SLOTS * NTILES, part_of_heads, 0)
    o_landed(0)
    forward(0).start()
    last = len(ORDER[-1]) - LAST
    take(ORDER[-1][:last])
    o_landed(1)
    forward(1).start()
    take(ORDER[-1][last:])
    r_local.wait()
    r_sib.wait_recv()
    g_sib.wait_recv()
    all_landed(ob.at[0:2, 0], f_recv)

    wide = outv.shape[3]
    parts = outv.shape[0]

    def out_cols(n):
        return pl.ds(pl.multiple_of(core * half + n * wide, 128), wide)

    def out_own(n):
        return pltpu.make_async_copy(outv.at[n, core], out.at[0, :, out_cols(n)], p_loc)

    def out_sib(n):
        return remote(outv.at[n, other], out.at[0, :, out_cols(n)], p_send, p_recv, sib)

    per_slot = wb.shape[0] // SLOTS
    depth = per_slot * wb.shape[1]

    def project(i, _):
        n = (i + z_lo) % parts
        cols = pl.ds(pl.multiple_of(n * wide, 128), wide)
        acc = None
        for slot in range(SLOTS):
            part = jnp.dot(
                ob[slot].reshape(NCORE * tok, depth),
                wb[slot * per_slot : (slot + 1) * per_slot, :, cols].reshape(depth, wide),
                preferred_element_type=jnp.float32,
            )
            acc = part if acc is None else acc + part
        for clip in range(NCORE):
            rows = acc[clip * tok : (clip + 1) * tok]
            mixed = rb[clip, :, cols].astype(jnp.float32) + gb[clip, 0:1, cols] * rows
            outv[n, clip] = mixed.astype(jnp.bfloat16)
        out_own(n).start()
        out_sib(n).start()
        return 0

    far = NCORE * NZ_HI * (NY - 1)

    def project_in_turn(i, _):
        @pl.when(i == parts - 1)
        def _():
            all_landed(wb.at[0:far, :, 0:SHARED], b_recv)

        return project(i, 0)

    lax.fori_loop(0, parts, project_in_turn, 0)

    for n in range(3):
        all_sent(kb.at[0:2, 0 : GROUP - 1], a_send.at[n])
    all_sent(stage.at[0:2, 0 : GROUP - 1], o_send)
    all_sent(ob.at[0:2, 0], f_send)
    all_sent(wb.at[0 : 3 * NCORE], z_send)
    all_sent(wb.at[0 : (NCORE * NZ_HI - 1) * (NY - 1), :, 0 : half - SHARED], y_send)
    all_sent(wb.at[0 : NY - 1, :, 0 : half - SHARED], x_send)
    all_sent(wb.at[0:far, :, 0:SHARED], b_send)
    w_sib.wait_send()
    r_sib.wait_send()
    g_sib.wait_send()
    pltpu.make_async_copy(outv.at[:, 0], outv.at[:, 0], p_loc).wait()
    all_sent(outv.at[:, 0], p_send)
    all_landed(outv.at[:, 0], p_recv)


def hand_over(strips, block, out, held, in_sem, out_sem):
    rows = block.shape[1] // strips
    copies = []
    for n in range(strips):
        part = (0, pl.ds(n * rows, rows))
        copies.append(
            (
                pltpu.make_async_copy(block.at[part], held.at[part], in_sem.at[n]),
                pltpu.make_async_copy(held.at[part], out.at[part], out_sem.at[n]),
            )
        )
    for load, _ in copies:
        load.start()
    for load, store in copies:
        load.wait()
        store.start()
    for _, store in copies:
        store.wait()


def on_device(
    query_rows, key_rows, value_rows, key_tiles, tile_counts, out_weight, gate_scale, residual
):
    tok, feats = query_rows.shape[1:]
    w_rows, width = out_weight.shape
    half = width // NCORE
    parts = half // SHARED
    bf16, f32 = jnp.bfloat16, jnp.float32
    dma = pltpu.SemaphoreType.DMA
    shards = NZ_HI * NY * NCORE
    hbm = pl.BlockSpec(memory_space=pltpu.HBM)
    vmem = pl.BlockSpec(memory_space=pltpu.VMEM)
    block_out = pl.pallas_call(
        kernel,
        out_shape=jax.ShapeDtypeStruct(residual.shape, residual.dtype),
        in_specs=[hbm, hbm, hbm, hbm, hbm, hbm, vmem, hbm],
        out_specs=pl.BlockSpec(memory_space=pl.ANY),
        scratch_shapes=[
            pltpu.SMEM((NTILES, NTILES, feats // HEAD_DIM), jnp.int32),
            pltpu.SMEM((NTILES, feats // HEAD_DIM), jnp.int32),
            pltpu.VMEM((SLOTS, GROUP, tok, HEAD_DIM), bf16),
            pltpu.VMEM((SLOTS, GROUP, tok, HEAD_DIM), bf16),
            pltpu.VMEM((SLOTS, GROUP, tok, HEAD_DIM), bf16),
            pltpu.VMEM((SLOTS, GROUP, tok, HEAD_DIM), bf16),
            pltpu.VMEM((SLOTS, NCORE, tok, feats // SLOTS), bf16),
            pltpu.VMEM((shards, w_rows, half), bf16),
            pltpu.VMEM((NCORE, tok, half), bf16),
            pltpu.VMEM((8, width), f32),
            pltpu.VMEM((NCORE, 8, half), f32),
            pltpu.VMEM((parts, NCORE, tok, half // parts), bf16),
            dma((3,)),
            dma((SLOTS, 3)),
            dma((SLOTS,)),
            dma,
            dma((SLOTS,)),
            dma((SLOTS,)),
            dma,
            dma,
            dma,
            dma((shards,)),
            dma,
            dma((2, 4)),
            dma,
            dma,
            dma,
            dma((3, NCORE)),
            dma((3,)),
            dma((3,)),
            dma((3,)),
            dma((2,)),
            dma,
            dma,
            dma,
        ],
        compiler_params=pltpu.CompilerParams(
            collective_id=0, has_side_effects=True, vmem_limit_bytes=56 << 20
        ),
    )(
        query_rows, key_rows, value_rows, jnp.transpose(key_tiles, (1, 2, 0)), tile_counts.T,
        out_weight, gate_scale, residual,
    )
    strips = 4
    return pl.pallas_call(
        functools.partial(hand_over, strips),
        out_shape=jax.ShapeDtypeStruct(residual.shape, residual.dtype),
        in_specs=[hbm],
        out_specs=pl.BlockSpec(memory_space=pl.ANY),
        scratch_shapes=[
            pltpu.VMEM(residual.shape, residual.dtype),
            dma((strips,)),
            dma((strips,)),
        ],
    )(block_out)


def solution(mesh):
    in_specs = (
        P("dp", "seq", None),
        P("dp", "seq", None),
        P("dp", "seq", None),
        P(),
        P(),
        P("dp", None),
        P("dp", None),
        P("dp", "seq", None),
    )
    return jax.shard_map(
        on_device, mesh=mesh, in_specs=in_specs, out_specs=P("dp", "seq", None), check_vma=False
    )
```

```python
import functools
import math

import jax
import jax.numpy as jnp
from jax import lax
from jax.experimental import pallas as pl
from jax.experimental.pallas import tpu as pltpu
from jax.sharding import PartitionSpec as P

MESH = pl.DeviceIdType.MESH

HEAD_DIM = 128
NX, NZ_LO = 4, 2
NY, NZ_HI, NCORE = 8, 4, 2
GROUP = NX * NZ_LO
SLOTS = 2
NTILES = 4
SHARED = (384, 384)
STEPS = ((4, 3, 4, 3), (3, 4, 3, 4))
LAST = 0
BESIDE = 1
ORDER = (
    (("y", 0, 0, 0, 0), ("y", 1, 0, 0, 0), ("z", 0, 0), ("y", 0, 0, 1, 0), ("y", 1, 0, 1, 0), ("z", 0, 1), ("f", 1, 0),
     ("y", 0, 0, 0, 1), ("y", 1, 0, 0, 1), ("z", 1, 0), ("f", 2, 0), ("y", 0, 1, 0, 0), ("y", 1, 1, 0, 0), ("z", 1, 1), ("f", 2, 1),
     ("y", 0, 0, 1, 1), ("y", 1, 0, 1, 1), ("y", 0, 0, 0, 2), ("y", 1, 0, 0, 2), ("z", 2, 0), ("f", 3, 0),
     ("y", 0, 2, 0, 0), ("y", 1, 2, 0, 0), ("y", 0, 1, 0, 1), ("y", 1, 1, 0, 1), ("z", 2, 1), ("f", 3, 1),
     ("y", 0, 2, 1, 0), ("y", 1, 2, 1, 0), ("y", 0, 0, 1, 2), ("y", 1, 0, 1, 2),),
    (("y", 0, 0, 0, 3), ("y", 1, 3, 0, 0),),
    (("y", 0, 3, 0, 0), ("y", 1, 2, 0, 1),),
    (("y", 0, 2, 0, 1), ("y", 1, 1, 0, 2), ("y", 0, 1, 0, 2), ("y", 1, 3, 1, 0),),
    (("y", 0, 3, 1, 0), ("y", 1, 2, 1, 1), ("y", 0, 2, 1, 1), ("y", 1, 3, 0, 1), ("y", 0, 0, 1, 3),
     ("y", 1, 2, 0, 2), ("x", 0, 0), ("x", 1, 0), ("y", 0, 3, 0, 1), ("y", 1, 1, 0, 3), ("x", 0, 1),
     ("x", 1, 1),),
    (("y", 0, 2, 0, 2), ("y", 1, 3, 1, 1),),
    (("y", 0, 3, 1, 1), ("y", 1, 2, 1, 2),),
    (("y", 0, 2, 1, 2), ("y", 1, 3, 0, 2), ("x", 1, 2), ("x", 0, 2), ("y", 0, 3, 0, 2), ("y", 1, 3, 1, 2),),
    (("x", 1, 3), ("y", 0, 2, 0, 3), ("y", 1, 3, 0, 3), ("y", 0, 3, 1, 2), ("y", 1, 3, 1, 3),
     ("y", 0, 2, 1, 3),),
)


def kernel(
    q_in, k_in, v_in, tiles_in, counts_in, w_in, gate_in, res_in, out,
    tiles, counts, qb, kb, vb, stage, ob, wb, rb, gs, gb, sums, outv,
    a_send, a_recv, a_loc, o_send, o_recv, o_loc, f_send, f_recv, y_send, y_recv, x_send, x_recv,
    b_send, b_recv, z_send, z_recv, s_send, s_recv, s_loc, t_loc, p_send, p_recv, p_loc,
):
    dp, me = lax.axis_index("dp"), lax.axis_index("seq")
    z_hi, y, core = dp // (NY * NCORE), (dp // NCORE) % NY, dp % NCORE
    z_lo, x = me // NX, me % NX
    way_z = 2 * z_lo - 1
    tok = q_in.shape[1]
    half = w_in.shape[1] // 2
    other = 1 - core

    sib = (dp + 1 - 2 * core, me)
    ring = tuple(
        (z_hi * NY * NCORE + ((y + d) % NY) * NCORE + core, me) for d in (1, NY - 1)
    )
    near = (((z_hi + way_z + NZ_HI) % NZ_HI) * NY * NCORE + y * NCORE + core, (1 - z_lo) * NX + x)
    twin = (dp, (1 - z_lo) * NX + x)
    beside = tuple((dp, z_lo * NX + (x + d) % NX) for d in (1, NX - 1))
    kept, skipped = 1 - x % 2, x % 2

    def peer(i):
        return ((z_lo + i // NX) % NZ_LO) * NX + (x + i) % NX

    def block_at(zh, yy):
        return ((yy // 2) % 2) * 16 + (zh * 2 + yy // 4) * 2 + yy % 2

    def shard_at(zh, yy, part):
        return block_at(zh, yy) * NCORE + (core + part) % NCORE

    def remote(src, dst, send, recv, to):
        return pltpu.make_async_remote_copy(
            src_ref=src, dst_ref=dst, send_sem=send, recv_sem=recv, device_id=to, device_id_type=MESH
        )

    def all_sent(view, sem):
        remote(view, view, sem, sem, sib).wait_send()

    def all_landed(view, sem):
        remote(view, view, sem, sem, sib).wait_recv()

    def head_cols(p, slot):
        return pl.ds(pl.multiple_of((p * SLOTS + slot) * HEAD_DIM, HEAD_DIM), HEAD_DIM)

    mine = pl.ds(pl.multiple_of(core * half, 128), half)
    theirs = pl.ds(pl.multiple_of(other * half, 128), half)
    orders = tuple(
        (z_hi + NZ_HI + off) % NZ_HI for off in (0, way_z, -way_z, 2)
    )
    y_cols = [pl.ds(pl.multiple_of(z_lo * n, 128), half - n) for n in SHARED]
    b_cols = [pl.ds(pl.multiple_of(z_lo * (half - n), 128), n) for n in SHARED]
    own_shard = shard_at(z_hi, y, 0)

    barrier = pltpu.get_barrier_semaphore()
    for to in (sib, *ring, near):
        pl.semaphore_signal(barrier, inc=1, device_id=to, device_id_type=MESH)

    def greet(i, _):
        pl.semaphore_signal(barrier, inc=1, device_id=(dp, peer(i)), device_id_type=MESH)
        return 0

    lax.fori_loop(1, GROUP, greet, 0)
    w_local = pltpu.make_async_copy(
        w_in.at[:, mine], wb.at[own_shard], s_loc.at[0]
    )
    w_local.start()
    tensors = ((k_in, kb), (v_in, vb), (q_in, qb))

    def own_copy(n, slot):
        src, dst = tensors[n]
        return pltpu.make_async_copy(src.at[0, :, head_cols(me, slot)], dst.at[slot, me], a_loc.at[slot])

    for slot in range(SLOTS):
        for n in range(3):
            own_copy(n, slot).start()
    t_local = pltpu.make_async_copy(tiles_in, tiles, t_loc.at[0])
    c_local = pltpu.make_async_copy(counts_in, counts, t_loc.at[1])
    t_local.start()
    c_local.start()
    r_local = pltpu.make_async_copy(res_in.at[0, :, mine], rb.at[core], s_loc.at[1])
    r_local.start()
    gs[...] = jnp.broadcast_to(gate_in[...].astype(jnp.float32), gs.shape)
    g_local = pltpu.make_async_copy(gs.at[:, mine], gb.at[core], s_loc.at[2])
    g_local.start()

    pl.semaphore_wait(barrier, GROUP + 3)

    w_sib = remote(
        w_in.at[:, theirs],
        wb.at[own_shard],
        s_send.at[0], s_recv.at[0], sib,
    )
    w_sib.start()

    def send_all(slot, lo, hi):
        for n in range(3):
            src, dst = tensors[n]

            def one(i, _, n=n, src=src, dst=dst):
                p = peer(i)
                if n == 2:
                    done = a_recv.at[slot, 1 + i // NX]
                else:
                    done = a_recv.at[slot, 0]
                remote(
                    src.at[0, :, head_cols(p, slot)], dst.at[slot, me], a_send.at[n], done, (dp, p)
                ).start()
                return 0

            lax.fori_loop(lo, hi, one, 0)

    def z_copy(n, part):
        view = wb.at[shard_at(orders[n], y, part)]
        return remote(view, view, z_send, z_recv.at[n, part], (near, twin, near)[n])

    def z_arrival(n, part):
        view = wb.at[shard_at(orders[n + 1], y, part)]
        return remote(view, view, z_send, z_recv.at[n, part], (near, twin, near)[n])

    def y_copy(way, j, at):
        view = wb.at[at, :, y_cols[j // 2]]
        return remote(view, view, y_send.at[j // 2], y_recv.at[at], ring[way])

    def x_copy(way, t, at):
        view = wb.at[at, :, y_cols[BESIDE // 2]]
        return remote(view, view, x_send, x_recv.at[way, t], beside[way])

    def b_copy(j, at):
        view = wb.at[at, :, b_cols[j // 2]]
        return remote(view, view, b_send.at[j // 2], b_recv.at[j // 2], near)

    def shard_of(j, yy, part):
        return shard_at(orders[j], yy, kept if j == BESIDE else part)

    def y_first(j, part):
        at = shard_of(j, y, part)
        for way in range(2):
            y_copy(way, j, at).start()

    def row_of(way, t):
        return (y + ((NY - 1 - t) if way == 0 else t + 1)) % NY

    def y_done(way, j, part, t):
        at = shard_of(j, row_of(way, t), part)
        y_copy(way, j, at).wait_recv()
        if t + 1 < STEPS[way][j]:
            y_copy(way, j, at).start()
        if j == BESIDE:
            x_copy(way, t, at).start()
        b_copy(j, at).start()

    def x_done(way, t):
        at = shard_at(orders[BESIDE], row_of(way, t), skipped)
        x_copy(way, t, at).wait_recv()
        b_copy(BESIDE, at).start()

    def z_done(n, part):
        z_arrival(n, part).wait_recv()
        if n < 2:
            z_copy(n + 1, part).start()
        if n == 0 and part:
            send_all(0, NX, GROUP)
            send_all(1, 1, GROUP)

    steps = {"f": y_first, "z": z_done, "y": y_done, "x": x_done}

    def take(group):
        for name, *where in group:
            steps[name](*where)

    w_local.wait()
    z_copy(0, 0).start()
    y_first(0, 0)
    send_all(0, 1, NX)
    w_sib.wait_recv()
    z_copy(0, 1).start()
    y_first(0, 1)
    r_sib = remote(res_in.at[0, :, theirs], rb.at[core], s_send.at[1], s_recv.at[1], sib)
    r_sib.start()
    g_local.wait()
    g_sib = remote(gs.at[:, theirs], gb.at[core], s_send.at[2], s_recv.at[2], sib)
    g_sib.start()

    def o_copy(slot, p):
        return remote(
            stage.at[slot, p], ob.at[slot, core, :, pl.ds(pl.multiple_of(me * HEAD_DIM, HEAD_DIM), HEAD_DIM)],
            o_send, o_recv.at[slot], (dp, p),
        )

    def o_own(slot):
        return pltpu.make_async_copy(
            stage.at[slot, me],
            ob.at[slot, core, :, pl.ds(pl.multiple_of(me * HEAD_DIM, HEAD_DIM), HEAD_DIM)],
            o_loc.at[slot],
        )

    factor = math.log2(math.e) / math.sqrt(HEAD_DIM)
    per_tile = GROUP // NTILES
    tile = per_tile * tok

    def attend(slot, q_tile):
        head = me * SLOTS + slot
        count = counts[q_tile, head]
        listed = [tiles[q_tile, n, head] for n in range(NTILES)]
        first = q_tile * per_tile
        queries = qb[slot, pl.ds(first, per_tile)].reshape(tile, HEAD_DIM)
        scores, peaks, seen = [], [], []
        for t in range(NTILES):
            keys = kb[slot, t * per_tile : (t + 1) * per_tile].reshape(tile, HEAD_DIM)
            s = lax.dot_general(
                queries, keys, (((1,), (1,)), ((), ())), preferred_element_type=jnp.float32
            )
            scores.append(s)
            peaks.append(jnp.max(s, axis=1, keepdims=True))
            hits = jnp.int32(0)
            for n in range(NTILES):
                hits = hits + jnp.where((listed[n] == t) & (n < count), 1, 0)
            seen.append(hits > 0)
        peak = None
        for t in range(NTILES):
            here = jnp.where(seen[t], peaks[t], -jnp.inf)
            peak = here if peak is None else jnp.maximum(peak, here)
        total, mixed = None, None
        for t in range(NTILES):
            shift = jnp.where(seen[t], peak * factor, jnp.inf)
            weights = jnp.exp2(scores[t] * factor - shift)
            values = vb[slot, t * per_tile : (t + 1) * per_tile].reshape(tile, HEAD_DIM)
            part = jnp.dot(weights.astype(jnp.bfloat16), values, preferred_element_type=jnp.float32)
            row = jnp.sum(weights, axis=1, keepdims=True)
            total = row if total is None else total + row
            mixed = part if mixed is None else mixed + part
        done = (mixed / total).astype(jnp.bfloat16)
        stage[slot, pl.ds(first, per_tile)] = done.reshape(per_tile, tok, HEAD_DIM)

    def part_of_heads(g, _):
        slot, c = g // NTILES, g % NTILES

        @pl.when(c == 0)
        def _():
            here = qb.at[0, 0:3]
            pltpu.make_async_copy(here, here, a_loc.at[slot]).wait()
            all_landed(kb.at[0:2, 0 : GROUP - 1], a_recv.at[slot, 0])
            all_landed(qb.at[0, 0 : NX - 1], a_recv.at[slot, 1])

        @pl.when(c == NTILES // 2)
        def _():
            all_landed(qb.at[0, 0:NX], a_recv.at[slot, 2])

        q_tile = ((z_lo + c // 2) % NZ_LO) * (NTILES // NZ_LO) + (x // per_tile + c) % (NTILES // NZ_LO)
        attend(slot, q_tile)
        for n in range(per_tile):
            p = q_tile * per_tile + n

            @pl.when(p != me)
            def _(p=p):
                o_copy(slot, p).start()

        for group in range(SLOTS * NTILES):

            @pl.when(g == group)
            def _(group=group):
                if group % NTILES == 0:
                    o_own(group // NTILES).start()
                if group < SLOTS * NTILES - 1:
                    take(ORDER[group + 1])

        return 0

    def o_landed(slot):
        all_landed(stage.at[slot, 0 : GROUP - 1], o_recv.at[slot])
        o_own(slot).wait()

    def forward(slot):
        view = ob.at[slot, core]
        return remote(view, view, f_send, f_recv, sib)

    take(ORDER[0])
    t_local.wait()
    c_local.wait()
    lax.fori_loop(0, SLOTS * NTILES, part_of_heads, 0)
    o_landed(0)
    forward(0).start()
    last = len(ORDER[-1]) - LAST
    take(ORDER[-1][:last])
    o_landed(1)
    forward(1).start()
    take(ORDER[-1][last:])
    r_local.wait()
    r_sib.wait_recv()
    g_sib.wait_recv()
    all_landed(ob.at[0:2, 0], f_recv)

    wide = outv.shape[3]
    parts = outv.shape[0]

    def out_cols(n):
        return pl.ds(pl.multiple_of(core * half + n * wide, 128), wide)

    def out_own(n):
        return pltpu.make_async_copy(outv.at[n, core], out.at[0, :, out_cols(n)], p_loc)

    def out_sib(n):
        return remote(outv.at[n, other], out.at[0, :, out_cols(n)], p_send, p_recv, sib)

    per_slot = wb.shape[0] // SLOTS
    depth = per_slot * wb.shape[1]

    per_zh = per_slot // NZ_HI
    zh_depth = per_zh * wb.shape[1]

    def out_cols_at(i):
        n = (i + z_lo) % parts
        return n, pl.ds(pl.multiple_of(n * wide, 128), wide)

    def finish(n, cols, acc):
        for clip in range(NCORE):
            rows = acc[clip * tok : (clip + 1) * tok]
            mixed = rb[clip, :, cols].astype(jnp.float32) + gb[clip, 0:1, cols] * rows
            outv[n, clip] = mixed.astype(jnp.bfloat16)
        out_own(n).start()
        out_sib(n).start()

    def project(i, _):
        n, cols = out_cols_at(i)
        acc = None
        for slot in range(SLOTS):
            part = jnp.dot(
                ob[slot].reshape(NCORE * tok, depth),
                wb[slot * per_slot : (slot + 1) * per_slot, :, cols].reshape(depth, wide),
                preferred_element_type=jnp.float32,
            )
            acc = part if acc is None else acc + part
        finish(n, cols, acc)
        return 0

    def products(places, cols):
        acc = None
        for j in places:
            zh = orders[j]
            feats = pl.ds(pl.multiple_of(zh * zh_depth, 128), zh_depth)
            for slot in range(SLOTS):
                part = jnp.dot(
                    ob[slot, :, :, feats].reshape(NCORE * tok, zh_depth),
                    wb[pl.ds(slot * per_slot + zh * per_zh, per_zh), :, cols].reshape(zh_depth, wide),
                    preferred_element_type=jnp.float32,
                )
                acc = part if acc is None else acc + part
        return acc

    far = NCORE * NZ_HI * (NY - 1) // 2
    all_landed(wb.at[0:far, :, 0 : SHARED[0]], b_recv.at[0])

    lax.fori_loop(0, parts - 1, project, 0)
    last_n, last_cols = out_cols_at(parts - 1)
    sums[...] = products((0, 1), last_cols)
    all_landed(wb.at[0:far, :, 0 : SHARED[1]], b_recv.at[1])
    finish(last_n, last_cols, sums[...] + products((2, 3), last_cols))

    for n in range(3):
        all_sent(kb.at[0:2, 0 : GROUP - 1], a_send.at[n])
    all_sent(stage.at[0:2, 0 : GROUP - 1], o_send)
    all_sent(ob.at[0:2, 0], f_send)
    all_sent(wb.at[0 : 3 * NCORE], z_send)
    for n in range(2):
        taken = far - (NY - 1) * (n == BESIDE // 2)
        all_sent(wb.at[0:taken, :, 0 : half - SHARED[n]], y_send.at[n])
        all_sent(wb.at[0:far, :, 0 : SHARED[n]], b_send.at[n])
    all_sent(wb.at[0 : NY - 1, :, 0 : half - SHARED[BESIDE // 2]], x_send)
    w_sib.wait_send()
    r_sib.wait_send()
    g_sib.wait_send()
    pltpu.make_async_copy(outv.at[:, 0], outv.at[:, 0], p_loc).wait()
    all_sent(outv.at[:, 0], p_send)
    all_landed(outv.at[:, 0], p_recv)


def hand_over(strips, block, out, held, in_sem, out_sem):
    rows = block.shape[1] // strips
    copies = []
    for n in range(strips):
        part = (0, pl.ds(n * rows, rows))
        copies.append(
            (
                pltpu.make_async_copy(block.at[part], held.at[part], in_sem.at[n]),
                pltpu.make_async_copy(held.at[part], out.at[part], out_sem.at[n]),
            )
        )
    for load, _ in copies:
        load.start()
    for load, store in copies:
        load.wait()
        store.start()
    for _, store in copies:
        store.wait()


def on_device(
    query_rows, key_rows, value_rows, key_tiles, tile_counts, out_weight, gate_scale, residual
):
    tok, feats = query_rows.shape[1:]
    w_rows, width = out_weight.shape
    half = width // NCORE
    parts = half // SHARED[1]
    bf16, f32 = jnp.bfloat16, jnp.float32
    dma = pltpu.SemaphoreType.DMA
    shards = NZ_HI * NY * NCORE
    hbm = pl.BlockSpec(memory_space=pltpu.HBM)
    vmem = pl.BlockSpec(memory_space=pltpu.VMEM)
    block_out = pl.pallas_call(
        kernel,
        out_shape=jax.ShapeDtypeStruct(residual.shape, residual.dtype),
        in_specs=[hbm, hbm, hbm, hbm, hbm, hbm, vmem, hbm],
        out_specs=pl.BlockSpec(memory_space=pl.ANY),
        scratch_shapes=[
            pltpu.SMEM((NTILES, NTILES, feats // HEAD_DIM), jnp.int32),
            pltpu.SMEM((NTILES, feats // HEAD_DIM), jnp.int32),
            pltpu.VMEM((SLOTS, GROUP, tok, HEAD_DIM), bf16),
            pltpu.VMEM((SLOTS, GROUP, tok, HEAD_DIM), bf16),
            pltpu.VMEM((SLOTS, GROUP, tok, HEAD_DIM), bf16),
            pltpu.VMEM((SLOTS, GROUP, tok, HEAD_DIM), bf16),
            pltpu.VMEM((SLOTS, NCORE, tok, feats // SLOTS), bf16),
            pltpu.VMEM((shards, w_rows, half), bf16),
            pltpu.VMEM((NCORE, tok, half), bf16),
            pltpu.VMEM((8, width), f32),
            pltpu.VMEM((NCORE, 8, half), f32),
            pltpu.VMEM((NCORE * tok, half // parts), f32),
            pltpu.VMEM((parts, NCORE, tok, half // parts), bf16),
            dma((3,)),
            dma((SLOTS, 3)),
            dma((SLOTS,)),
            dma,
            dma((SLOTS,)),
            dma((SLOTS,)),
            dma,
            dma,
            dma((2,)),
            dma((shards,)),
            dma,
            dma((2, 4)),
            dma((2,)),
            dma((2,)),
            dma,
            dma((3, NCORE)),
            dma((3,)),
            dma((3,)),
            dma((3,)),
            dma((2,)),
            dma,
            dma,
            dma,
        ],
        compiler_params=pltpu.CompilerParams(
            collective_id=0, has_side_effects=True, vmem_limit_bytes=56 << 20
        ),
    )(
        query_rows, key_rows, value_rows, jnp.transpose(key_tiles, (1, 2, 0)), tile_counts.T,
        out_weight, gate_scale, residual,
    )
    strips = 4
    return pl.pallas_call(
        functools.partial(hand_over, strips),
        out_shape=jax.ShapeDtypeStruct(residual.shape, residual.dtype),
        in_specs=[hbm],
        out_specs=pl.BlockSpec(memory_space=pl.ANY),
        scratch_shapes=[
            pltpu.VMEM(residual.shape, residual.dtype),
            dma((strips,)),
            dma((strips,)),
        ],
    )(block_out)


def solution(mesh):
    in_specs = (
        P("dp", "seq", None),
        P("dp", "seq", None),
        P("dp", "seq", None),
        P(),
        P(),
        P("dp", None),
        P("dp", None),
        P("dp", "seq", None),
    )
    return jax.shard_map(
        on_device, mesh=mesh, in_specs=in_specs, out_specs=P("dp", "seq", None), check_vma=False
    )
```
